32 devices in a mesh: tm: 4 (over y, core), space: 8 (over z, x).
Axes of the slice: x: 2, y: 2, z: 4, core: 2. Of those that a mesh axis runs over, the one named last changes fastest.
Arguments:
- initial: float32 [4, 3, 8, 16, 16, 128], P('tm', None, 'space'), may hold values from -3 to 3
Outputs:
- end_state: float32 [4, 3, 8, 16, 16, 128], P('tm', None, 'space')
The draws below stay inside these ranges and needn't reach their ends.
All inputs are finite; a program needn't handle non-finite values.
Results may differ from the reference program's by a relative error of at most 0.0001.
Values sent between devices are 32-bit elements; how exact they have to be, the bound alone decides.
A program may use at most 128 MiB of HBM per device.

```python
import jax
import jax.numpy as jnp
import numpy as np
from jax import lax

SIDE = 16
YBRICKS = 4
ZCELLS = 128
BRICKS = 8
SLICES = 4
N_TM = 4


def steps_of(rng, shape, split, smallest, high):
    level, own = 1.0, jax.random.fold_in(rng, 6)
    for dim, blocks in split:
        heights = jnp.exp(jax.random.uniform(jax.random.fold_in(own, dim), (blocks,), jnp.float32, smallest / len(split), high / len(split)))
        level = level * jnp.repeat(heights, shape[dim] // blocks).reshape([-1 if axis == dim else 1 for axis in range(len(shape))])
    return level


def scatter_about(own_key, extent, deviation, limit, cuts=(), kind=jnp.bfloat16):
    entries = deviation * jax.random.normal(own_key, extent, jnp.float32)
    if cuts:
        entries = entries * steps_of(own_key, extent, cuts, -0.22, 0.18)
    return jnp.clip(entries, -limit, limit).astype(kind)


def setup_inputs(seed: int = 0) -> dict:
    key_of = jax.random.split(jax.random.key(seed), 2)
    initial = scatter_about(key_of[0], (SLICES, 3, BRICKS, SIDE, SIDE, ZCELLS), 0.5, 3.0, ((0, 4), (2, 8)), jnp.float32)
    return {"initial": initial}


EXACT = lax.Precision.HIGHEST
TIME_STEP = 0.001
VISCOSITY = 0.05
QUAD_WEIGHTS = ((5.0 / 24.0, 1.0 / 3.0, -1.0 / 24.0), (-1.0 / 24.0, 1.0 / 3.0, 5.0 / 24.0))


def cheb_tables(count):
    index = np.arange(count)
    points = -np.cos(np.pi * index / (count - 1))
    weights = (-1.0) ** index
    weights[0] = weights[0] * 0.5
    weights[-1] = weights[-1] * 0.5
    return points, weights


def diff_matrix(points, weights):
    count = points.shape[0]
    ident = np.eye(count)
    gaps = points[:, None] - points[None, :] + ident
    matrix = (weights[None, :] / weights[:, None]) / gaps
    matrix = matrix * (1.0 - ident)
    return matrix - ident * matrix.sum(axis=1)[:, None]


def interp_matrix(points, weights, targets):
    gaps = targets[:, None] - points[None, :]
    exact_hit = np.abs(gaps) < 1e-12
    safe_gaps = np.where(exact_hit, 1.0, gaps)
    terms = weights[None, :] / safe_gaps
    matrix = terms / terms.sum(axis=1, keepdims=True)
    any_hit = exact_hit.any(axis=1)
    return np.where(any_hit[:, None], np.where(exact_hit, 1.0, 0.0), matrix)


def apply_along(values, matrix, axis):
    full_shape = values.shape
    rows_out, rows_in = matrix.shape
    elements = full_shape[axis] // rows_in
    blocked = values.reshape(full_shape[:axis] + (elements, rows_in) + full_shape[axis + 1:])
    einsum_forms = {1: "ij,cejyz->ceiyz", 2: "ij,cxejz->cxeiz", 3: "ij,cxyej->cxyei"}
    result = jnp.einsum(einsum_forms[axis], matrix, blocked, precision=EXACT)
    return result.reshape(full_shape[:axis] + (elements * rows_out,) + full_shape[axis + 1:])


def derivative(values, axis, diff, lift_coef):
    count = diff.shape[0]
    length = values.shape[axis]
    position = jnp.arange(length) % count
    bshape = [1, 1, 1, 1]
    bshape[axis] = length
    is_first = (position == 0).astype(jnp.float32).reshape(bshape)
    is_last = (position == count - 1).astype(jnp.float32).reshape(bshape)
    inner = apply_along(values, diff, axis)
    return inner + lift_coef * (is_first * (values - jnp.roll(values, 1, axis)) + is_last * (jnp.roll(values, -1, axis) - values))


def tendency(field, diff, lift_coef):
    grad_x = derivative(field, 1, diff, lift_coef)
    grad_y = derivative(field, 2, diff, lift_coef)
    grad_z = derivative(field, 3, diff, lift_coef)
    advect = -(field[0:1] * grad_x + field[1:2] * grad_y + field[2:3] * grad_z)
    viscous = derivative(grad_x, 1, diff, lift_coef) + derivative(grad_y, 2, diff, lift_coef) + derivative(grad_z, 3, diff, lift_coef)
    return advect + VISCOSITY * viscous


def quadrature(rates, which):
    weight_row = QUAD_WEIGHTS[which]
    return weight_row[0] * rates[0] + weight_row[1] * rates[1] + weight_row[2] * rates[2]


def sdc_sweep(start, old_rates, start_rate, rate_fn, fas_terms, need_last):
    states = [start]
    rates = [start_rate]
    for which in range(2):
        advanced = states[which] + (TIME_STEP / 2.0) * (rates[which] - old_rates[which]) + TIME_STEP * quadrature(old_rates, which)
        if fas_terms is not None:
            advanced = advanced + fas_terms[which]
        states.append(advanced)
        if which == 0 or need_last:
            rates.append(rate_fn(advanced))
    return states, rates


def bricks_to_grid(field):
    chans, bricks, side, unused_side, depth = field.shape
    rows = bricks // YBRICKS
    blocked = field.reshape(chans, rows, YBRICKS, side, side, depth).transpose(0, 1, 3, 2, 4, 5)
    return blocked.reshape(chans, rows * side, YBRICKS * side, depth)


def grid_to_bricks(field, side):
    chans, width_x, width_y, depth = field.shape
    rows = width_x // side
    blocked = field.reshape(chans, rows, side, YBRICKS, side, depth).transpose(0, 1, 3, 2, 4, 5)
    return blocked.reshape(chans, rows * YBRICKS, side, side, depth)


def reference(initial):
    fine_points, fine_weights = cheb_tables(16)
    coarse_points, coarse_weights = cheb_tables(8)
    fine_diff = jnp.asarray(diff_matrix(fine_points, fine_weights), jnp.float32)
    coarse_diff = jnp.asarray(diff_matrix(coarse_points, coarse_weights), jnp.float32)
    restrict_mat = jnp.asarray(interp_matrix(fine_points, fine_weights, coarse_points), jnp.float32)
    prolong_mat = jnp.asarray(interp_matrix(coarse_points, coarse_weights, fine_points), jnp.float32)
    fine_lift = 15.0 ** 2 / 2.0
    coarse_lift = 7.0 ** 2 / 2.0
    side = initial.shape[3]

    def fine_rate(field):
        return tendency(field, fine_diff, fine_lift)

    def coarse_rate(field):
        return tendency(field, coarse_diff, coarse_lift)

    def restrict(field):
        return apply_along(apply_along(apply_along(field, restrict_mat, 1), restrict_mat, 2), restrict_mat, 3)

    def prolong(field):
        return apply_along(apply_along(apply_along(field, prolong_mat, 3), prolong_mat, 2), prolong_mat, 1)

    results = []
    prev_coarse = None
    prev_fine = None
    for slice_index in range(N_TM):
        start_state = bricks_to_grid(initial[slice_index])
        first_rate = fine_rate(start_state)
        fine_one, fine_rates = sdc_sweep(start_state, [first_rate, first_rate, first_rate], first_rate, fine_rate, None, True)
        coarse_nodes = [restrict(state) for state in fine_one]
        coarse_rates = [coarse_rate(state) for state in coarse_nodes]
        fas_terms = [restrict(TIME_STEP * quadrature(fine_rates, which)) - TIME_STEP * quadrature(coarse_rates, which) for which in range(2)]
        if slice_index == 0:
            coarse_start = restrict(start_state)
            fine_start = start_state
        else:
            coarse_start = prev_coarse
            fine_start = prev_fine
        coarse_out, unused_rates = sdc_sweep(coarse_start, coarse_rates, coarse_rate(coarse_start), coarse_rate, fas_terms, False)
        prev_coarse = coarse_out[2]
        prev_fine = fine_one[2]
        node_zero = fine_start + prolong(coarse_out[0] - restrict(fine_start))
        node_one = fine_one[1] + prolong(coarse_out[1] - coarse_nodes[1])
        node_two = fine_one[2] + prolong(coarse_out[2] - coarse_nodes[2])
        new_rates = [fine_rate(node_zero), fine_rate(node_one), fine_rate(node_two)]
        fine_two, unused_fine = sdc_sweep(node_zero, new_rates, new_rates[0], fine_rate, None, False)
        results.append(grid_to_bricks(fine_two[2], side))
    return jnp.stack(results)
```

```python
import functools
import jax
import jax.numpy as jnp
import numpy as np
from jax import lax
from jax.experimental import pallas as pl
from jax.experimental.pallas import tpu as pltpu
from jax.sharding import PartitionSpec as P

YBRICKS = 4
FINE = 16
COARSE = 8
LANES = 128
TIME_STEP = 0.001
VISCOSITY = 0.05
QUAD_WEIGHTS = ((5.0 / 24.0, 1.0 / 3.0, -1.0 / 24.0), (-1.0 / 24.0, 1.0 / 3.0, 5.0 / 24.0))
MESH = pl.DeviceIdType.MESH
F32 = jnp.float32
BF16 = jnp.bfloat16


def cheb_tables(count):
    index = np.arange(count)
    points = -np.cos(np.pi * index / (count - 1))
    weights = (-1.0) ** index
    weights[0] = weights[0] * 0.5
    weights[-1] = weights[-1] * 0.5
    return (points, weights)


def diff_matrix(points, weights):
    count = points.shape[0]
    ident = np.eye(count)
    gaps = points[:, None] - points[None, :] + ident
    matrix = weights[None, :] / weights[:, None] / gaps
    matrix = matrix * (1.0 - ident)
    return matrix - ident * matrix.sum(axis=1)[:, None]


def interp_matrix(points, weights, targets):
    gaps = targets[:, None] - points[None, :]
    exact_hit = np.abs(gaps) < 1e-12
    safe_gaps = np.where(exact_hit, 1.0, gaps)
    terms = weights[None, :] / safe_gaps
    matrix = terms / terms.sum(axis=1, keepdims=True)
    any_hit = exact_hit.any(axis=1)
    return np.where(any_hit[:, None], np.where(exact_hit, 1.0, 0.0), matrix)


def lifted_matrix(count, length, periodic):
    points, weights = cheb_tables(count)
    matrix = np.kron(np.eye(length // count), diff_matrix(points, weights))
    lift_coef = (count - 1) ** 2 / 2.0
    for place in range(length):
        if place % count == 0:
            matrix[place, place] += lift_coef
            if place > 0:
                matrix[place, place - 1] -= lift_coef
            elif periodic:
                matrix[place, length - 1] -= lift_coef
        if place % count == count - 1:
            matrix[place, place] -= lift_coef
            if place < length - 1:
                matrix[place, place + 1] += lift_coef
            elif periodic:
                matrix[place, 0] += lift_coef
    return matrix


def halves(matrix):
    high = np.asarray(matrix, np.float32).astype(jnp.bfloat16)
    low = (np.asarray(matrix, np.float64) - high.astype(np.float64)).astype(np.float32).astype(jnp.bfloat16)
    return high, low


def left_table(matrix):
    high, low = halves(matrix)
    return np.concatenate([high, high, low], axis=1)


def right_table(matrix):
    high, low = halves(matrix)
    return np.concatenate([high, high, low], axis=0)


def padded(matrix, rows, columns):
    return np.pad(matrix, ((0, rows - matrix.shape[0]), (0, columns - matrix.shape[1])))


def level_tables(count, side, z_length, lanes):
    brick = lifted_matrix(count, side, False)
    lift = (count - 1) ** 2 / 2.0
    ident = np.eye(side)
    first, last = ident[:, :1], ident[:, -1:]
    second = brick @ brick - lift**2 * (first @ first.T + last @ last.T)
    along_x = lambda m: np.kron(m, ident)
    along_y = lambda m: np.kron(ident, m)
    inner = np.concatenate(
        [along_x(brick), along_y(brick), VISCOSITY * (along_x(second) + along_y(second))]
    )
    faces = np.concatenate(
        [form(m) for form in (along_x, along_y) for e in (first, last) for m in (e.T, e.T @ brick)]
    )
    grad_cols, visc_cols = [], []
    for e, sign in ((first, -lift), (last, lift)):
        grad_cols += [sign * e, 0.0 * e]
        visc_cols += [VISCOSITY * sign * (brick @ e), VISCOSITY * sign * e]
    nothing = [0.0 * first] * 4
    rows = lambda cx, cy: np.concatenate([along_x(m) for m in cx] + [along_y(m) for m in cy], axis=1)
    outer = np.concatenate(
        [rows(grad_cols, nothing), rows(nothing, grad_cols), rows(visc_cols, visc_cols)]
    )
    depth = lifted_matrix(count, z_length, True)
    depth_t = np.concatenate(
        [padded(depth.T, lanes, lanes), padded(VISCOSITY * (depth @ depth).T, lanes, lanes)], axis=1
    )
    return [left_table(inner), left_table(faces), left_table(outer), right_table(depth_t)]


def split(value):
    high = value.astype(BF16)
    low = (value - high.astype(F32)).astype(BF16)
    return high, low


def stacked(value):
    high, low = split(value)
    return jnp.concatenate([high, low, high], axis=0)


def left(table, value3):
    return jnp.dot(table[...], value3, preferred_element_type=F32)


def right(value, table, lanes):
    high, low = split(value)
    blocks = []
    for at in range(0, value.shape[1], lanes):
        h, l = high[:, at : at + lanes], low[:, at : at + lanes]
        blocks.append(jnp.concatenate([h, l, h], axis=1))
    return jnp.dot(jnp.concatenate(blocks, axis=0), table[...], preferred_element_type=F32)


def unstack(value, rows):
    return jnp.concatenate([value[at : at + rows] for at in range(0, value.shape[0], rows)], axis=1)


def kernel(geometry, q_ref, *refs):
    slices, bricks, fine_rows, coarse_rows, lanes = geometry
    tables, refs = refs[:12], refs[12:]
    fine_tab, coarse_tab = tables[:4], tables[4:8]
    restrict_rows, restrict_z, prolong_rows, prolong_z = tables[8:]
    out_ref, refs = refs[0], refs[1:]
    (v1, v2, start, rates, nodes, f_send, f_recv, f_acc, c_send, c_recv, c_acc, seq, terms, saved,
     f_ssem, f_rsem, c_ssem, c_rsem, t_ssem, t_rsem, s_ssem, s_rsem) = refs

    p = lax.axis_index("tm")
    b = lax.axis_index("space")
    column = lax.rem(b, YBRICKS)
    base = b - column
    x_low = lax.rem(b + bricks - YBRICKS, bricks)
    x_high = lax.rem(b + YBRICKS, bricks)
    y_low = base + lax.rem(column + YBRICKS - 1, YBRICKS)
    y_high = base + lax.rem(column + 1, YBRICKS)
    targets = (x_low, x_high, y_low, y_high)
    landing = (1, 0, 3, 2)

    barrier = pltpu.get_barrier_semaphore()
    for target in targets:
        pl.semaphore_signal(barrier, inc=1, device_id={"space": target}, device_id_type=MESH)
    for k in range(1, slices):
        pl.semaphore_signal(
            barrier, inc=1, device_id={"tm": lax.rem(p + k, slices)}, device_id_type=MESH
        )
    pl.semaphore_wait(barrier, 4 + slices - 1)

    def copies(send, recv, ssem, rsem, slot):
        size = send.shape[1] // 4
        return [
            pltpu.make_async_remote_copy(
                src_ref=send.at[slot, pl.ds(d * size, size)],
                dst_ref=recv.at[slot, pl.ds(landing[d] * size, size)],
                send_sem=ssem.at[slot, d],
                recv_sem=rsem.at[slot, landing[d]],
                device_id={"space": targets[d]},
                device_id_type=MESH,
            )
            for d in range(4)
        ]

    fine_part = (f_send, f_recv, f_ssem, f_rsem)
    coarse_part = (c_send, c_recv, c_ssem, c_rsem)

    def begin(value, tab, part, slot):
        value3 = stacked(value)
        part[0][slot] = left(tab[1], value3)
        for copy in copies(*part, slot):
            copy.start()
        return value3

    def local(value, value3, tab, acc):
        rows = value.shape[0]
        acc[:, : 3 * lanes] = left(tab[0], value3)
        deep = right(value, tab[3], lanes)
        for c in range(3):
            at = slice(c * lanes, (c + 1) * lanes)
            one = deep[c * rows : (c + 1) * rows]
            acc[:rows, 3 * lanes + c * lanes : 4 * lanes + c * lanes] = one[:, :lanes]
            acc[2 * rows :, at] += one[:, lanes:]

    def finish(value, tab, part, slot, acc):
        rows = value.shape[0]
        for copy in copies(*part, slot):
            copy.wait()
        total = acc[:, : 3 * lanes] + left(tab[2], stacked(part[1][slot]))
        out = []
        for c in range(3):
            at = slice(c * lanes, (c + 1) * lanes)
            deep = acc[:rows, 3 * lanes + c * lanes : 4 * lanes + c * lanes]
            out.append(
                total[2 * rows :, at]
                - (
                    value[:, :lanes] * total[:rows, at]
                    + value[:, lanes : 2 * lanes] * total[rows : 2 * rows, at]
                    + value[:, 2 * lanes :] * deep
                )
            )
        return jnp.concatenate(out, axis=1)

    def restrict(value):
        less = left(restrict_rows, stacked(value))
        return unstack(right(less, restrict_z, lanes), coarse_rows)

    def prolong(value):
        deep = unstack(right(value, prolong_z, lanes), coarse_rows)
        return left(prolong_rows, stacked(deep))

    h = TIME_STEP
    q = jnp.concatenate([q_ref[c] for c in range(3)], axis=1)
    q3 = begin(q, fine_tab, fine_part, 0)
    local(q, q3, fine_tab, f_acc)
    saved[0] = restrict(q)
    seq[0] = saved[0]
    rates[0] = finish(q, fine_tab, fine_part, 0, f_acc)

    v1[...] = q + (0.5 * h) * rates[0]
    w3 = begin(v1[...], fine_tab, fine_part, 1)
    saved[1] = restrict(v1[...])
    c0 = begin(saved[0], coarse_tab, coarse_part, 0)
    c1 = begin(saved[1], coarse_tab, coarse_part, 1)
    local(v1[...], w3, fine_tab, f_acc)
    rates[1] = finish(v1[...], fine_tab, fine_part, 1, f_acc)
    v2[...] = v1[...] + (0.5 * h) * rates[1]
    w3 = begin(v2[...], fine_tab, fine_part, 2)

    def hand_on():
        return pltpu.make_async_remote_copy(
            src_ref=v2,
            dst_ref=start,
            send_sem=s_ssem,
            recv_sem=s_rsem,
            device_id={"tm": lax.rem(p + 1, slices)},
            device_id_type=MESH,
        )

    @pl.when(p + 1 < slices)
    def _():
        hand_on().start()

    @pl.when(p == 0)
    def _():
        for c in range(3):
            start[:, c * lanes : (c + 1) * lanes] = q_ref[c]

    local(v2[...], w3, fine_tab, f_acc)
    for m, value3 in ((0, c0), (1, c1)):
        local(saved[m], value3, coarse_tab, c_acc)
        saved[3 + m] = finish(saved[m], coarse_tab, coarse_part, m, c_acc)
    saved[2] = restrict(v2[...])
    known = [restrict(rates[0]), restrict(rates[1])]
    known.append(restrict(finish(v2[...], fine_tab, fine_part, 2, f_acc)))
    for m in range(2):
        row = QUAD_WEIGHTS[m]
        mixed = h * (row[0] * known[0] + row[1] * known[1] + row[2] * known[2])
        if m == 0:
            terms[2 * p] = mixed + jnp.where(p == 0, saved[0], (-0.5 * h) * saved[3])
        else:
            terms[2 * p + 1] = mixed - (0.5 * h) * saved[4]

    def term_copy(source, k):
        return pltpu.make_async_remote_copy(
            src_ref=terms.at[pl.ds(2 * source, 2)],
            dst_ref=terms.at[pl.ds(2 * source, 2)],
            send_sem=t_ssem.at[k],
            recv_sem=t_rsem.at[source],
            device_id={"tm": lax.rem(p + k, slices)},
            device_id_type=MESH,
        )

    for k in range(slices - 1, 0, -1):
        @pl.when(p + k < slices)
        def _():
            term_copy(p, k).start()

    @pl.when(p > 0)
    def _():
        hand_on().wait_recv()

    saved[5] = restrict(start[...])

    @pl.when(p > 0)
    def _():
        term_copy(0, 1).wait_recv()

    seq[1] = terms[0]

    def stage(r, carry):
        value = seq[r + 1]
        value3 = begin(value, coarse_tab, coarse_part, r + 2)
        local(value, value3, coarse_tab, c_acc)
        source = (r + 1) // 2

        @pl.when((r % 2 == 1) & (source < p))
        def _():
            term_copy(source, 1).wait_recv()

        rate = finish(value, coarse_tab, coarse_part, r + 2, c_acc)
        seq[r + 2] = value + (0.5 * h) * rate + terms[r + 1]
        return carry

    lax.fori_loop(0, 2 * p + 1, stage, 0)

    for k in range(1, slices):
        @pl.when(p + k < slices)
        def _():
            term_copy(p, k).wait_send()

    @pl.when(p + 1 < slices)
    def _():
        hand_on().wait_send()

    values3 = []
    for m, (whole, part) in enumerate(((start, saved.at[5]), (v1, saved.at[1]), (v2, saved.at[2]))):
        nodes[m] = whole[...] + prolong(seq[2 * p + m] - part[...])
        values3.append(begin(nodes[m], fine_tab, fine_part, 3 + m))
    for m in range(3):
        local(nodes[m], values3[m], fine_tab, f_acc)
        rates[m] = finish(nodes[m], fine_tab, fine_part, 3 + m, f_acc)

    row = QUAD_WEIGHTS[0]
    v1[...] = nodes[0] + h * (row[0] * rates[0] + row[1] * rates[1] + row[2] * rates[2])
    w3 = begin(v1[...], fine_tab, fine_part, 6)
    local(v1[...], w3, fine_tab, f_acc)
    row = QUAD_WEIGHTS[1]
    v2[...] = v1[...] + h * (row[0] * rates[0] + (row[1] - 0.5) * rates[1] + row[2] * rates[2])
    last = v2[...] + (0.5 * h) * finish(v1[...], fine_tab, fine_part, 6, f_acc)
    for c in range(3):
        out_ref[c] = last[:, c * lanes : (c + 1) * lanes]


def solution(mesh):
    slices, bricks = mesh.shape["tm"], mesh.shape["space"]

    def shards(initial):
        side, z_length = initial.shape[3], initial.shape[-1]
        lanes = z_length
        half = side // 2
        fine_rows, coarse_rows = side * side, half * half
        fine_points, fine_weights = cheb_tables(FINE)
        coarse_points, coarse_weights = cheb_tables(COARSE)
        down = interp_matrix(fine_points, fine_weights, coarse_points)
        up = interp_matrix(coarse_points, coarse_weights, fine_points)
        spread = lambda m, length: np.kron(np.eye(length // m.shape[1]), m)
        down_side, up_side = spread(down, side), spread(up, half)
        tables = (
            level_tables(FINE, side, z_length, lanes)
            + level_tables(COARSE, half, z_length // 2, lanes)
            + [
                left_table(np.kron(down_side, down_side)),
                right_table(padded(spread(down, z_length).T, lanes, lanes)),
                left_table(np.kron(up_side, up_side)),
                right_table(padded(spread(up, z_length // 2).T, lanes, lanes)),
            ]
        )
        wide = 3 * lanes
        fine_slots, coarse_slots = 7, 2 * slices + 1
        fine_field = pltpu.VMEM((fine_rows, wide), F32)
        geometry = (slices, bricks, fine_rows, coarse_rows, lanes)
        result = pl.pallas_call(
            functools.partial(kernel, geometry),
            out_shape=jax.ShapeDtypeStruct((3, fine_rows, lanes), F32),
            in_specs=[pl.BlockSpec(memory_space=pltpu.VMEM)] * (1 + len(tables)),
            out_specs=pl.BlockSpec(memory_space=pltpu.VMEM),
            scratch_shapes=[
                fine_field,
                fine_field,
                fine_field,
                pltpu.VMEM((3, fine_rows, wide), F32),
                pltpu.VMEM((3, fine_rows, wide), F32),
                pltpu.VMEM((fine_slots, 8 * side, wide), F32),
                pltpu.VMEM((fine_slots, 8 * side, wide), F32),
                pltpu.VMEM((3 * fine_rows, 2 * wide), F32),
                pltpu.VMEM((coarse_slots, 8 * half, wide), F32),
                pltpu.VMEM((coarse_slots, 8 * half, wide), F32),
                pltpu.VMEM((3 * coarse_rows, 2 * wide), F32),
                pltpu.VMEM((2 * slices + 1, coarse_rows, wide), F32),
                pltpu.VMEM((2 * slices, coarse_rows, wide), F32),
                pltpu.VMEM((6, coarse_rows, wide), F32),
                pltpu.SemaphoreType.DMA((fine_slots, 4)),
                pltpu.SemaphoreType.DMA((fine_slots, 4)),
                pltpu.SemaphoreType.DMA((coarse_slots, 4)),
                pltpu.SemaphoreType.DMA((coarse_slots, 4)),
                pltpu.SemaphoreType.DMA((slices,)),
                pltpu.SemaphoreType.DMA((slices,)),
                pltpu.SemaphoreType.DMA,
                pltpu.SemaphoreType.DMA,
            ],
            compiler_params=pltpu.CompilerParams(
                collective_id=0, has_side_effects=True, vmem_limit_bytes=40 * 2**20
            ),
        )(initial.reshape(3, fine_rows, lanes), *[jnp.asarray(t) for t in tables])
        return result.reshape(initial.shape)

    return jax.shard_map(
        shards,
        mesh=mesh,
        in_specs=(P("tm", None, "space", None, None, None),),
        out_specs=P("tm", None, "space", None, None, None),
        check_vma=False,
    )
```

```python
import functools
import jax
import jax.numpy as jnp
import numpy as np
from jax import lax
from jax.experimental import pallas as pl
from jax.experimental.pallas import tpu as pltpu
from jax.sharding import PartitionSpec as P

YBRICKS = 4
FINE = 16
COARSE = 8
LANES = 128
TIME_STEP = 0.001
VISCOSITY = 0.05
QUAD_WEIGHTS = ((5.0 / 24.0, 1.0 / 3.0, -1.0 / 24.0), (-1.0 / 24.0, 1.0 / 3.0, 5.0 / 24.0))
MESH = pl.DeviceIdType.MESH
F32 = jnp.float32
BF16 = jnp.bfloat16


def cheb_tables(count):
    index = np.arange(count)
    points = -np.cos(np.pi * index / (count - 1))
    weights = (-1.0) ** index
    weights[0] = weights[0] * 0.5
    weights[-1] = weights[-1] * 0.5
    return (points, weights)


def diff_matrix(points, weights):
    count = points.shape[0]
    ident = np.eye(count)
    gaps = points[:, None] - points[None, :] + ident
    matrix = weights[None, :] / weights[:, None] / gaps
    matrix = matrix * (1.0 - ident)
    return matrix - ident * matrix.sum(axis=1)[:, None]


def interp_matrix(points, weights, targets):
    gaps = targets[:, None] - points[None, :]
    exact_hit = np.abs(gaps) < 1e-12
    safe_gaps = np.where(exact_hit, 1.0, gaps)
    terms = weights[None, :] / safe_gaps
    matrix = terms / terms.sum(axis=1, keepdims=True)
    any_hit = exact_hit.any(axis=1)
    return np.where(any_hit[:, None], np.where(exact_hit, 1.0, 0.0), matrix)


def lifted_matrix(count, length, periodic):
    points, weights = cheb_tables(count)
    matrix = np.kron(np.eye(length // count), diff_matrix(points, weights))
    lift_coef = (count - 1) ** 2 / 2.0
    for place in range(length):
        if place % count == 0:
            matrix[place, place] += lift_coef
            if place > 0:
                matrix[place, place - 1] -= lift_coef
            elif periodic:
                matrix[place, length - 1] -= lift_coef
        if place % count == count - 1:
            matrix[place, place] -= lift_coef
            if place < length - 1:
                matrix[place, place + 1] += lift_coef
            elif periodic:
                matrix[place, 0] += lift_coef
    return matrix


def halves(matrix):
    high = np.asarray(matrix, np.float32).astype(jnp.bfloat16)
    low = (np.asarray(matrix, np.float64) - high.astype(np.float64)).astype(np.float32).astype(jnp.bfloat16)
    return high, low


def left_table(matrix):
    high, low = halves(matrix)
    return np.concatenate([high, high, low], axis=1)


def right_table(matrix):
    high, low = halves(matrix)
    return np.concatenate([high, high, low], axis=0)


def padded(matrix, rows, columns):
    return np.pad(matrix, ((0, rows - matrix.shape[0]), (0, columns - matrix.shape[1])))


def face_rows(brick, side, packed):
    ident = np.eye(side)
    ends = (ident[:1], ident[-1:])
    forms = (lambda m: np.kron(m, ident), lambda m: np.kron(ident, m))
    value = [form(e) for form in forms for e in ends]
    slope = [form(e @ brick) for form in forms for e in ends]
    if packed:
        return value + slope
    return [m for pair in zip(value, slope) for m in pair]


def level_tables(count, side, z_length, lanes, packed):
    brick = lifted_matrix(count, side, False)
    lift = (count - 1) ** 2 / 2.0
    ident = np.eye(side)
    first, last = ident[:, :1], ident[:, -1:]
    second = brick @ brick - lift**2 * (first @ first.T + last @ last.T)
    along_x = lambda m: np.kron(m, ident)
    along_y = lambda m: np.kron(ident, m)
    inner = np.concatenate(
        [along_x(brick), along_y(brick), VISCOSITY * (along_x(second) + along_y(second))]
    )
    faces = np.concatenate(face_rows(brick, side, packed))
    grad_cols, visc_cols = [], []
    for e, sign in ((first, -lift), (last, lift)):
        grad_cols += [sign * e, 0.0 * e]
        visc_cols += [VISCOSITY * sign * (brick @ e), VISCOSITY * sign * e]
    nothing = [0.0 * first] * 4
    order = [0, 2, 4, 6, 1, 3, 5, 7] if packed else list(range(8))

    def rows(cx, cy):
        columns = [along_x(m) for m in cx] + [along_y(m) for m in cy]
        return np.concatenate([columns[i] for i in order], axis=1)

    outer = np.concatenate(
        [rows(grad_cols, nothing), rows(nothing, grad_cols), rows(visc_cols, visc_cols)]
    )
    depth = lifted_matrix(count, z_length, True)
    twice = lanes // z_length
    depth_t = np.concatenate(
        [np.tile(m.T, (1, twice)) for m in (depth, VISCOSITY * (depth @ depth))], axis=1
    )
    depth_t = padded(depth_t, lanes, 2 * lanes)
    return [left_table(inner), left_table(faces), left_table(outer), right_table(depth_t)]


def split(value):
    high = value.astype(BF16)
    low = (value - high.astype(F32)).astype(BF16)
    return high, low


def stacked(value):
    high, low = split(value)
    return jnp.concatenate([high, low, high], axis=0)


def left(table, value3):
    return jnp.dot(table[...], value3, preferred_element_type=F32)


def right(value, table, lanes):
    high, low = split(value)
    blocks = []
    for at in range(0, value.shape[1], lanes):
        h, l = high[:, at : at + lanes], low[:, at : at + lanes]
        blocks.append(jnp.concatenate([h, l, h], axis=1))
    return jnp.dot(jnp.concatenate(blocks, axis=0), table[...], preferred_element_type=F32)


def unstack(value, rows):
    return jnp.concatenate([value[at : at + rows] for at in range(0, value.shape[0], rows)], axis=1)


def kernel(geometry, table_count, q_hbm, *refs):
    slices, bricks, fine_rows, coarse_rows, lanes = geometry
    sources, refs = refs[:table_count], refs[table_count:]
    out_ref, q_ref, refs = refs[0], refs[1], refs[2:]
    tables, refs = refs[:table_count], refs[table_count:]
    fine_tab, coarse_tab = tables[:4], tables[4:8]
    (restrict_rows, restrict_z, prolong_rows, prolong_z,
     delta_faces, halo_z, halo_rows) = tables[8:]
    (l_sem, v1, v2, start, start_halo, rates, nodes, f_send, f_recv, f_acc, c_send, c_recv, c_acc,
     seq, terms, saved, f_ssem, f_rsem, c_ssem, c_rsem, t_ssem, t_rsem, s_ssem, s_rsem) = refs
    half = lanes // 2
    size = c_send.shape[1]

    q_load = pltpu.make_async_copy(q_hbm, q_ref, l_sem.at[table_count])
    q_load.start()
    loads = {}
    for i in (1, 0, 3, 2, 8, 9, 5, 4, 7, 6, 10, 11, 12, 13, 14):
        loads[i] = pltpu.make_async_copy(sources[i], tables[i], l_sem.at[i])
        loads[i].start()

    p = lax.axis_index("tm")
    b = lax.axis_index("space")
    column = lax.rem(b, YBRICKS)
    base = b - column
    x_low = lax.rem(b + bricks - YBRICKS, bricks)
    x_high = lax.rem(b + YBRICKS, bricks)
    y_low = base + lax.rem(column + YBRICKS - 1, YBRICKS)
    y_high = base + lax.rem(column + 1, YBRICKS)
    targets = (x_low, x_high, y_low, y_high)
    landing = (1, 0, 3, 2)

    barrier = pltpu.get_barrier_semaphore()
    for target in targets:
        pl.semaphore_signal(barrier, inc=1, device_id={"space": target}, device_id_type=MESH)
    for k in range(1, slices):
        pl.semaphore_signal(
            barrier, inc=1, device_id={"tm": lax.rem(p + k, slices)}, device_id_type=MESH
        )
    pl.semaphore_wait(barrier, 4 + slices - 1)

    def copies(send, recv, ssem, rsem, slot):
        size = send.shape[1] // 4
        return [
            pltpu.make_async_remote_copy(
                src_ref=send.at[slot, pl.ds(d * size, size)],
                dst_ref=recv.at[slot, pl.ds(landing[d] * size, size)],
                send_sem=ssem.at[slot, d],
                recv_sem=rsem.at[slot, landing[d]],
                device_id={"space": targets[d]},
                device_id_type=MESH,
            )
            for d in range(4)
        ]

    fine_part = (f_send, f_recv, f_ssem, f_rsem)
    coarse_part = (c_send, c_recv, c_ssem, c_rsem)
    low_lanes = lax.broadcasted_iota(jnp.int32, (size, 3 * lanes), 1) % lanes < half

    def begin(value3, slot):
        f_send[slot] = left(fine_tab[1], value3)
        for copy in copies(*fine_part, slot):
            copy.start()

    def coarse_begin(value3, table, slot):
        faces = left(table, value3)
        c_send[slot] = jnp.where(low_lanes, faces[:size], faces[size:])
        for copy in copies(*coarse_part, slot):
            copy.start()

    def arrive(part, slot):
        for copy in copies(*part, slot):
            copy.wait()
        return part[1][slot]

    def local(value, value3, tab, acc):
        rows = value.shape[0]
        acc[:, : 3 * lanes] = left(tab[0], value3)
        deep = right(value, tab[3], lanes)
        for c in range(3):
            at = slice(c * lanes, (c + 1) * lanes)
            one = deep[c * rows : (c + 1) * rows]
            acc[:rows, 3 * lanes + c * lanes : 4 * lanes + c * lanes] = one[:, :lanes]
            acc[2 * rows :, at] += one[:, lanes:]

    def finish(value, tab, halo, acc):
        rows = value.shape[0]
        total = acc[:, : 3 * lanes] + left(tab[2], stacked(halo))
        out = []
        for c in range(3):
            at = slice(c * lanes, (c + 1) * lanes)
            deep = acc[:rows, 3 * lanes + c * lanes : 4 * lanes + c * lanes]
            out.append(
                total[2 * rows :, at]
                - (
                    value[:, :lanes] * total[:rows, at]
                    + value[:, lanes : 2 * lanes] * total[rows : 2 * rows, at]
                    + value[:, 2 * lanes :] * deep
                )
            )
        return jnp.concatenate(out, axis=1)

    def coarse_finish(value, slot, acc):
        got = arrive(coarse_part, slot)
        turned = jnp.concatenate(
            [pltpu.roll(got[:, c * lanes : (c + 1) * lanes], half, 1) for c in range(3)], axis=1
        )
        halo = jnp.concatenate(
            [jnp.where(low_lanes, got, turned), jnp.where(low_lanes, turned, got)], axis=0
        )
        return finish(value, coarse_tab, halo, acc)

    def restrict(value3):
        return unstack(right(left(restrict_rows, value3), restrict_z, lanes), coarse_rows)

    def prolong(value):
        deep = unstack(right(value, prolong_z, lanes), coarse_rows)
        return left(prolong_rows, stacked(deep))

    def prolong_halo(got):
        both = right(got, halo_z, lanes)
        parts = [unstack(both[:, :lanes], size), unstack(both[:, lanes:], size)]
        return left(halo_rows, stacked(jnp.concatenate(parts, axis=0)))

    h = TIME_STEP
    q_load.wait()
    q = jnp.concatenate([q_ref[c] for c in range(3)], axis=1)
    value3 = stacked(q)
    loads[1].wait()
    begin(value3, 0)
    for i in (0, 3):
        loads[i].wait()
    local(q, value3, fine_tab, f_acc.at[0])
    for i in (2, 8, 9):
        loads[i].wait()
    saved[0] = restrict(value3)
    seq[0] = saved[0]
    rates[0] = finish(q, fine_tab, arrive(fine_part, 0), f_acc.at[0])

    v1[...] = q + (0.5 * h) * rates[0]
    value3 = stacked(v1[...])
    begin(value3, 1)
    saved[1] = restrict(value3)
    for i in (4, 5, 6, 7, 10, 11, 12, 13, 14):
        loads[i].wait()
    for m in range(2):
        coarse3 = stacked(saved[m])
        coarse_begin(coarse3, coarse_tab[1], m)
        local(saved[m], coarse3, coarse_tab, c_acc.at[m])
    local(v1[...], value3, fine_tab, f_acc.at[0])
    rates[1] = finish(v1[...], fine_tab, arrive(fine_part, 1), f_acc.at[0])
    v2[...] = v1[...] + (0.5 * h) * rates[1]
    value3 = stacked(v2[...])
    begin(value3, 2)

    def hand_on(source, target, which):
        return pltpu.make_async_remote_copy(
            src_ref=source,
            dst_ref=target,
            send_sem=s_ssem.at[which],
            recv_sem=s_rsem.at[which],
            device_id={"tm": lax.rem(p + 1, slices)},
            device_id_type=MESH,
        )

    handed = lambda: (hand_on(v2, start, 0), hand_on(f_recv.at[2], start_halo, 1))

    @pl.when(p + 1 < slices)
    def _():
        handed()[0].start()

    @pl.when(p == 0)
    def _():
        for c in range(3):
            start[:, c * lanes : (c + 1) * lanes] = q_ref[c]
        start_halo[...] = f_recv[0]

    local(v2[...], value3, fine_tab, f_acc.at[0])
    for m in range(2):
        saved[3 + m] = coarse_finish(saved[m], m, c_acc.at[m])
    saved[2] = restrict(value3)
    known = [restrict(stacked(rates[0])), restrict(stacked(rates[1]))]
    known.append(restrict(stacked(finish(v2[...], fine_tab, arrive(fine_part, 2), f_acc.at[0]))))
    for m in range(2):
        row = QUAD_WEIGHTS[m]
        mixed = h * (row[0] * known[0] + row[1] * known[1] + row[2] * known[2])
        if m == 0:
            terms[2 * p] = mixed + jnp.where(p == 0, saved[0], (-0.5 * h) * saved[3])
        else:
            terms[2 * p + 1] = mixed - (0.5 * h) * saved[4]

    def term_copy(source, k):
        return pltpu.make_async_remote_copy(
            src_ref=terms.at[pl.ds(2 * source, 2)],
            dst_ref=terms.at[pl.ds(2 * source, 2)],
            send_sem=t_ssem.at[k],
            recv_sem=t_rsem.at[source],
            device_id={"tm": lax.rem(p + k, slices)},
            device_id_type=MESH,
        )

    for k in range(slices - 1, 0, -1):
        @pl.when(p + k < slices)
        def _():
            term_copy(p, k).start()

    @pl.when(p + 1 < slices)
    def _():
        handed()[1].start()

    @pl.when(p > 0)
    def _():
        handed()[0].wait_recv()

    saved[5] = restrict(stacked(start[...]))

    @pl.when(p > 0)
    def _():
        term_copy(0, 1).wait_recv()

    seq[1] = terms[0]

    def advance(value, r):
        rate = coarse_finish(value, r + 2, c_acc.at[0])
        seq[r + 2] = value + (0.5 * h) * rate + terms[r + 1]

    def open_stage(r):
        value = seq[r + 1]
        value3 = stacked(value)
        coarse_begin(value3, coarse_tab[1], r + 2)
        local(value, value3, coarse_tab, c_acc.at[0])
        return value

    def stage(r, carry):
        value = open_stage(r)
        source = (r + 1) // 2

        @pl.when((r % 2 == 1) & (source < p))
        def _():
            term_copy(source, 1).wait_recv()

        advance(value, r)
        return carry

    lax.fori_loop(0, 2 * p, stage, 0)
    value = open_stage(2 * p)

    @pl.when(p > 0)
    def _():
        handed()[1].wait_recv()

    wholes = ((start, saved.at[5]), (v1, saved.at[1]), (v2, saved.at[2]))

    def correct(m):
        whole, part = wholes[m]
        delta = seq[2 * p + m] - part[...]
        coarse_begin(stacked(delta), delta_faces, 2 * slices + 1 + m)
        nodes[m] = whole[...] + prolong(delta)

    for m in range(2):
        correct(m)
    advance(value, 2 * p)
    correct(2)
    for m in range(3):
        local(nodes[m], stacked(nodes[m]), fine_tab, f_acc.at[m])
    for m, base_halo in enumerate((start_halo, f_recv.at[1], f_recv.at[2])):
        got = arrive(coarse_part, 2 * slices + 1 + m)
        rates[m] = finish(nodes[m], fine_tab, base_halo[...] + prolong_halo(got), f_acc.at[m])

    for k in range(1, slices):
        @pl.when(p + k < slices)
        def _():
            term_copy(p, k).wait_send()

    @pl.when(p + 1 < slices)
    def _():
        for copy in handed():
            copy.wait_send()

    row = QUAD_WEIGHTS[0]
    v1[...] = nodes[0] + h * (row[0] * rates[0] + row[1] * rates[1] + row[2] * rates[2])
    value3 = stacked(v1[...])
    begin(value3, 3)
    local(v1[...], value3, fine_tab, f_acc.at[0])
    row = QUAD_WEIGHTS[1]
    v2[...] = v1[...] + h * (row[0] * rates[0] + (row[1] - 0.5) * rates[1] + row[2] * rates[2])
    last = v2[...] + (0.5 * h) * finish(v1[...], fine_tab, arrive(fine_part, 3), f_acc.at[0])
    for c in range(3):
        out_ref[c] = last[:, c * lanes : (c + 1) * lanes]


def solution(mesh):
    slices, bricks = mesh.shape["tm"], mesh.shape["space"]

    def shards(initial):
        side, z_length = initial.shape[3], initial.shape[-1]
        lanes = z_length
        half = side // 2
        fine_rows, coarse_rows = side * side, half * half
        fine_points, fine_weights = cheb_tables(FINE)
        coarse_points, coarse_weights = cheb_tables(COARSE)
        down = interp_matrix(fine_points, fine_weights, coarse_points)
        up = interp_matrix(coarse_points, coarse_weights, fine_points)
        spread = lambda m, length: np.kron(np.eye(length // m.shape[1]), m)
        down_side, up_side = spread(down, side), spread(up, half)
        fine_brick = lifted_matrix(FINE, side, False)
        slope_of = [fine_brick[:1] @ up_side, fine_brick[-1:] @ up_side]
        ident = np.eye(half)
        delta_slopes = [np.kron(m, ident) for m in slope_of] + [np.kron(ident, m) for m in slope_of]
        delta_values = face_rows(np.eye(half), half, True)[:4]
        spots = np.eye(8)
        halo_table = np.concatenate(
            [np.kron(spots[j : j + 1], up_side) for d in range(4) for j in (d, 4 + d)]
        )
        up_z = spread(up, z_length // 2).T
        down_z = spread(down, z_length).T
        tables = (
            level_tables(FINE, side, z_length, lanes, False)
            + level_tables(COARSE, half, z_length // 2, lanes, True)
            + [
                left_table(np.kron(down_side, down_side)),
                right_table(np.tile(down_z, (1, 2))),
                left_table(np.kron(up_side, up_side)),
                right_table(padded(up_z, lanes, lanes)),
                left_table(np.concatenate(delta_values + delta_slopes)),
                right_table(np.kron(np.eye(2), up_z)),
                left_table(halo_table),
            ]
        )
        wide = 3 * lanes
        fine_slots, coarse_slots = 4, 2 * slices + 4
        fine_field = pltpu.VMEM((fine_rows, wide), F32)
        geometry = (slices, bricks, fine_rows, coarse_rows, lanes)
        result = pl.pallas_call(
            functools.partial(kernel, geometry, len(tables)),
            out_shape=jax.ShapeDtypeStruct((3, fine_rows, lanes), F32),
            in_specs=[pl.BlockSpec(memory_space=pltpu.HBM)] * (1 + len(tables)),
            out_specs=pl.BlockSpec(memory_space=pltpu.VMEM),
            scratch_shapes=[pltpu.VMEM((3, fine_rows, lanes), F32)]
            + [pltpu.VMEM(t.shape, BF16) for t in tables]
            + [
                pltpu.SemaphoreType.DMA((len(tables) + 1,)),
                fine_field,
                fine_field,
                fine_field,
                pltpu.VMEM((8 * side, wide), F32),
                pltpu.VMEM((3, fine_rows, wide), F32),
                pltpu.VMEM((3, fine_rows, wide), F32),
                pltpu.VMEM((fine_slots, 8 * side, wide), F32),
                pltpu.VMEM((fine_slots, 8 * side, wide), F32),
                pltpu.VMEM((3, 3 * fine_rows, 2 * wide), F32),
                pltpu.VMEM((coarse_slots, 4 * half, wide), F32),
                pltpu.VMEM((coarse_slots, 4 * half, wide), F32),
                pltpu.VMEM((2, 3 * coarse_rows, 2 * wide), F32),
                pltpu.VMEM((2 * slices + 1, coarse_rows, wide), F32),
                pltpu.VMEM((2 * slices, coarse_rows, wide), F32),
                pltpu.VMEM((6, coarse_rows, wide), F32),
                pltpu.SemaphoreType.DMA((fine_slots, 4)),
                pltpu.SemaphoreType.DMA((fine_slots, 4)),
                pltpu.SemaphoreType.DMA((coarse_slots, 4)),
                pltpu.SemaphoreType.DMA((coarse_slots, 4)),
                pltpu.SemaphoreType.DMA((slices,)),
                pltpu.SemaphoreType.DMA((slices,)),
                pltpu.SemaphoreType.DMA((2,)),
                pltpu.SemaphoreType.DMA((2,)),
            ],
            compiler_params=pltpu.CompilerParams(
                collective_id=0, has_side_effects=True, vmem_limit_bytes=48 * 2**20
            ),
        )(initial.reshape(3, fine_rows, lanes), *[jnp.asarray(t) for t in tables])
        return result.reshape(initial.shape)

    return jax.shard_map(
        shards,
        mesh=mesh,
        in_specs=(P("tm", None, "space", None, None, None),),
        out_specs=P("tm", None, "space", None, None, None),
        check_vma=False,
    )
```

```python
import functools
import jax
import jax.numpy as jnp
import numpy as np
from jax import lax
from jax.experimental import pallas as pl
from jax.experimental.pallas import tpu as pltpu
from jax.sharding import PartitionSpec as P

YBRICKS = 4
FINE = 16
COARSE = 8
LANES = 128
TIME_STEP = 0.001
VISCOSITY = 0.05
QUAD_WEIGHTS = ((5.0 / 24.0, 1.0 / 3.0, -1.0 / 24.0), (-1.0 / 24.0, 1.0 / 3.0, 5.0 / 24.0))
MESH = pl.DeviceIdType.MESH
F32 = jnp.float32
BF16 = jnp.bfloat16
VMEM_LIMIT = 62 * 2**20


def cheb_tables(count):
    index = np.arange(count)
    points = -np.cos(np.pi * index / (count - 1))
    weights = (-1.0) ** index
    weights[0] = weights[0] * 0.5
    weights[-1] = weights[-1] * 0.5
    return (points, weights)


def diff_matrix(points, weights):
    count = points.shape[0]
    ident = np.eye(count)
    gaps = points[:, None] - points[None, :] + ident
    matrix = weights[None, :] / weights[:, None] / gaps
    matrix = matrix * (1.0 - ident)
    return matrix - ident * matrix.sum(axis=1)[:, None]


def interp_matrix(points, weights, targets):
    gaps = targets[:, None] - points[None, :]
    exact_hit = np.abs(gaps) < 1e-12
    safe_gaps = np.where(exact_hit, 1.0, gaps)
    terms = weights[None, :] / safe_gaps
    matrix = terms / terms.sum(axis=1, keepdims=True)
    any_hit = exact_hit.any(axis=1)
    return np.where(any_hit[:, None], np.where(exact_hit, 1.0, 0.0), matrix)


def lifted_matrix(count, length, periodic):
    points, weights = cheb_tables(count)
    matrix = np.kron(np.eye(length // count), diff_matrix(points, weights))
    lift_coef = (count - 1) ** 2 / 2.0
    for place in range(length):
        if place % count == 0:
            matrix[place, place] += lift_coef
            if place > 0:
                matrix[place, place - 1] -= lift_coef
            elif periodic:
                matrix[place, length - 1] -= lift_coef
        if place % count == count - 1:
            matrix[place, place] -= lift_coef
            if place < length - 1:
                matrix[place, place + 1] += lift_coef
            elif periodic:
                matrix[place, 0] += lift_coef
    return matrix


def halves(matrix):
    high = np.asarray(matrix, np.float32).astype(jnp.bfloat16)
    low = (np.asarray(matrix, np.float64) - high.astype(np.float64)).astype(np.float32).astype(jnp.bfloat16)
    return high, low


def left_table(matrix):
    high, low = halves(matrix)
    return np.concatenate([high, high, low], axis=1)


def right_table(matrix):
    high, low = halves(matrix)
    return np.concatenate([high, high, low], axis=0)


def padded(matrix, rows, columns):
    return np.pad(matrix, ((0, rows - matrix.shape[0]), (0, columns - matrix.shape[1])))


def face_rows(brick, side, packed):
    ident = np.eye(side)
    ends = (ident[:1], ident[-1:])
    forms = (lambda m: np.kron(m, ident), lambda m: np.kron(ident, m))
    value = [form(e) for form in forms for e in ends]
    slope = [form(e @ brick) for form in forms for e in ends]
    if packed:
        return value + slope
    return [m for pair in zip(value, slope) for m in pair]


def level_tables(count, side, z_length, lanes, packed):
    brick = lifted_matrix(count, side, False)
    lift = (count - 1) ** 2 / 2.0
    ident = np.eye(side)
    first, last = ident[:, :1], ident[:, -1:]
    second = brick @ brick - lift**2 * (first @ first.T + last @ last.T)
    along_x = lambda m: np.kron(m, ident)
    along_y = lambda m: np.kron(ident, m)
    inner = np.concatenate(
        [along_x(brick), along_y(brick), VISCOSITY * (along_x(second) + along_y(second))]
    )
    faces = np.concatenate(face_rows(brick, side, packed))
    grad_cols, visc_cols = [], []
    for e, sign in ((first, -lift), (last, lift)):
        grad_cols += [sign * e, 0.0 * e]
        visc_cols += [VISCOSITY * sign * (brick @ e), VISCOSITY * sign * e]
    nothing = [0.0 * first] * 4
    order = [0, 2, 4, 6, 1, 3, 5, 7] if packed else list(range(8))

    def rows(cx, cy):
        columns = [along_x(m) for m in cx] + [along_y(m) for m in cy]
        return np.concatenate([columns[i] for i in order], axis=1)

    outer = np.concatenate(
        [rows(grad_cols, nothing), rows(nothing, grad_cols), rows(visc_cols, visc_cols)]
    )
    depth = lifted_matrix(count, z_length, True)
    twice = lanes // z_length
    depth_t = np.concatenate(
        [np.tile(m.T, (1, twice)) for m in (depth, VISCOSITY * (depth @ depth))], axis=1
    )
    depth_t = padded(depth_t, lanes, 2 * lanes)
    return [left_table(inner), left_table(faces), left_table(outer), right_table(depth_t)]


def split(value):
    high = value.astype(BF16)
    low = (value - high.astype(F32)).astype(BF16)
    return high, low


def stacked(value):
    high, low = split(value)
    return jnp.concatenate([high, low, high], axis=0)


def left(table, value3):
    return jnp.dot(table[:, : value3.shape[0]], value3, preferred_element_type=F32)


def right(value, table, lanes):
    high, low = split(value)
    blocks = []
    for at in range(0, value.shape[1], lanes):
        h, l = high[:, at : at + lanes], low[:, at : at + lanes]
        blocks.append(jnp.concatenate([h, l, h], axis=1))
    return jnp.dot(jnp.concatenate(blocks, axis=0), table[...], preferred_element_type=F32)


def unstack(value, rows):
    return jnp.concatenate([value[at : at + rows] for at in range(0, value.shape[0], rows)], axis=1)


def kernel(geometry, places, q_hbm, *refs):
    slices, bricks, fine_rows, coarse_rows, lanes = geometry
    table_count = len(places)
    sources, refs = refs[:2], refs[2:]
    out_ref, q_ref, refs = refs[0], refs[1], refs[2:]
    tables, refs = refs[:table_count], refs[table_count:]
    fine_tab, coarse_tab = tables[:4], tables[4:8]
    (restrict_rows, restrict_z, prolong_rows, prolong_z,
     delta_faces, halo_z, halo_rows) = tables[8:]
    (l_sem, v1, v2, start, start_halo, rates, nodes, f_send, f_recv, f_acc, c_send, c_recv, c_acc,
     seq, terms, saved, f_ssem, f_rsem, c_ssem, c_rsem, t_ssem, t_rsem, s_ssem, s_rsem) = refs
    half = lanes // 2
    size = c_send.shape[1]

    q_load = pltpu.make_async_copy(q_hbm, q_ref, l_sem.at[table_count])
    q_load.start()
    loads = {}
    for i in (1, 0, 3, 2, 8, 9, 5, 4, 7, 6, 10, 11, 12, 13, 14):
        bank, at = places[i]
        rows, columns = tables[i].shape
        loads[i] = pltpu.make_async_copy(
            sources[bank].at[pl.ds(at, rows), pl.ds(0, columns)], tables[i], l_sem.at[i]
        )
        loads[i].start()

    p = lax.axis_index("tm")
    b = lax.axis_index("space")
    column = lax.rem(b, YBRICKS)
    base = b - column
    x_low = lax.rem(b + bricks - YBRICKS, bricks)
    x_high = lax.rem(b + YBRICKS, bricks)
    y_low = base + lax.rem(column + YBRICKS - 1, YBRICKS)
    y_high = base + lax.rem(column + 1, YBRICKS)
    targets = (x_low, x_high, y_low, y_high)
    landing = (1, 0, 3, 2)

    barrier = pltpu.get_barrier_semaphore()
    for target in targets:
        pl.semaphore_signal(barrier, inc=1, device_id={"space": target}, device_id_type=MESH)
    for k in range(1, slices):
        pl.semaphore_signal(
            barrier, inc=1, device_id={"tm": lax.rem(p + k, slices)}, device_id_type=MESH
        )
    pl.semaphore_wait(barrier, 4 + slices - 1)

    def copies(send, recv, ssem, rsem, slot):
        size = send.shape[1] // 4
        return [
            pltpu.make_async_remote_copy(
                src_ref=send.at[slot, pl.ds(d * size, size)],
                dst_ref=recv.at[slot, pl.ds(landing[d] * size, size)],
                send_sem=ssem.at[slot, d],
                recv_sem=rsem.at[slot, landing[d]],
                device_id={"space": targets[d]},
                device_id_type=MESH,
            )
            for d in range(4)
        ]

    fine_part = (f_send, f_recv, f_ssem, f_rsem)
    coarse_part = (c_send, c_recv, c_ssem, c_rsem)
    low_lanes = lax.broadcasted_iota(jnp.int32, (size, 3 * lanes), 1) % lanes < half

    def begin(value3, slot):
        f_send[slot] = left(fine_tab[1], value3)
        for copy in copies(*fine_part, slot):
            copy.start()

    def coarse_begin(value3, table, slot):
        faces = left(table, value3)
        c_send[slot] = jnp.where(low_lanes, faces[:size], faces[size:])
        for copy in copies(*coarse_part, slot):
            copy.start()

    def arrive(part, slot):
        for copy in copies(*part, slot):
            copy.wait()
        return part[1][slot]

    def local(value, value3, tab, acc):
        rows = value.shape[0]
        acc[:, : 3 * lanes] = left(tab[0], value3)
        deep = right(value, tab[3], lanes)
        for c in range(3):
            at = slice(c * lanes, (c + 1) * lanes)
            one = deep[c * rows : (c + 1) * rows]
            acc[:rows, 3 * lanes + c * lanes : 4 * lanes + c * lanes] = one[:, :lanes]
            acc[2 * rows :, at] += one[:, lanes:]

    def finish(value, tab, halo, acc):
        rows = value.shape[0]
        total = acc[:, : 3 * lanes] + left(tab[2], stacked(halo))
        out = []
        for c in range(3):
            at = slice(c * lanes, (c + 1) * lanes)
            deep = acc[:rows, 3 * lanes + c * lanes : 4 * lanes + c * lanes]
            out.append(
                total[2 * rows :, at]
                - (
                    value[:, :lanes] * total[:rows, at]
                    + value[:, lanes : 2 * lanes] * total[rows : 2 * rows, at]
                    + value[:, 2 * lanes :] * deep
                )
            )
        return jnp.concatenate(out, axis=1)

    def coarse_finish(value, slot, acc):
        got = arrive(coarse_part, slot)
        turned = jnp.concatenate(
            [pltpu.roll(got[:, c * lanes : (c + 1) * lanes], half, 1) for c in range(3)], axis=1
        )
        halo = jnp.concatenate(
            [jnp.where(low_lanes, got, turned), jnp.where(low_lanes, turned, got)], axis=0
        )
        return finish(value, coarse_tab, halo, acc)

    def restrict(value3):
        return unstack(right(left(restrict_rows, value3), restrict_z, lanes), coarse_rows)

    def prolong(value):
        deep = unstack(right(value, prolong_z, lanes), coarse_rows)
        return left(prolong_rows, stacked(deep))

    def prolong_halo(got):
        both = right(got, halo_z, lanes)
        parts = [unstack(both[:, :lanes], size), unstack(both[:, lanes:], size)]
        return left(halo_rows, stacked(jnp.concatenate(parts, axis=0)))

    h = TIME_STEP
    q_load.wait()
    q = jnp.concatenate([q_ref[c] for c in range(3)], axis=1)
    value3 = stacked(q)
    loads[1].wait()
    begin(value3, 0)
    for i in (0, 3):
        loads[i].wait()
    local(q, value3, fine_tab, f_acc.at[0])
    for i in (2, 8, 9):
        loads[i].wait()
    saved[0] = restrict(value3)
    seq[0] = saved[0]
    rates[0] = finish(q, fine_tab, arrive(fine_part, 0), f_acc.at[0])

    v1[...] = q + (0.5 * h) * rates[0]
    value3 = stacked(v1[...])
    begin(value3, 1)
    saved[1] = restrict(value3)
    for i in (4, 5, 6, 7, 10, 11, 12, 13, 14):
        loads[i].wait()
    for m in range(2):
        coarse3 = stacked(saved[m])
        coarse_begin(coarse3, coarse_tab[1], m)
        local(saved[m], coarse3, coarse_tab, c_acc.at[m])
    local(v1[...], value3, fine_tab, f_acc.at[0])
    rates[1] = finish(v1[...], fine_tab, arrive(fine_part, 1), f_acc.at[0])
    v2[...] = v1[...] + (0.5 * h) * rates[1]
    value3 = stacked(v2[...])
    begin(value3, 2)

    def hand_on(source, target, which):
        return pltpu.make_async_remote_copy(
            src_ref=source,
            dst_ref=target,
            send_sem=s_ssem.at[which],
            recv_sem=s_rsem.at[which],
            device_id={"tm": lax.rem(p + 1, slices)},
            device_id_type=MESH,
        )

    hand_state = lambda: hand_on(v2, start, 0)
    hand_halo = lambda: hand_on(f_recv.at[2], start_halo, 1)

    @pl.when(p + 1 < slices)
    def _():
        hand_state().start()

    @pl.when(p == 0)
    def _():
        for c in range(3):
            start[:, c * lanes : (c + 1) * lanes] = q_ref[c]
        start_halo[...] = f_recv[0]

    local(v2[...], value3, fine_tab, f_acc.at[0])
    for m in range(2):
        saved[3 + m] = coarse_finish(saved[m], m, c_acc.at[m])
    saved[2] = restrict(value3)
    known = [restrict(stacked(rates[0])), restrict(stacked(rates[1]))]
    known.append(restrict(stacked(finish(v2[...], fine_tab, arrive(fine_part, 2), f_acc.at[0]))))
    first, second = [
        h * (row[0] * known[0] + row[1] * known[1] + row[2] * known[2]) for row in QUAD_WEIGHTS
    ]
    first = first + jnp.where(p == 0, saved[0], (-0.5 * h) * saved[3])
    second = second - (0.5 * h) * saved[4]
    low_field = lax.broadcasted_iota(jnp.int32, first.shape, 1) % lanes < half
    terms[p] = jnp.where(low_field, first, second)

    def term_copy(source, k):
        return pltpu.make_async_remote_copy(
            src_ref=terms.at[source],
            dst_ref=terms.at[source],
            send_sem=t_ssem.at[k],
            recv_sem=t_rsem.at[source],
            device_id={"tm": lax.rem(p + k, slices)},
            device_id_type=MESH,
        )

    for k in range(slices - 1, 0, -1):
        @pl.when(p + k < slices)
        def _():
            term_copy(p, k).start()

    @pl.when(p > 0)
    def _():
        term_copy(0, 1).wait_recv()

    def term(source, which):
        both = terms[source]
        turned = jnp.concatenate(
            [pltpu.roll(both[:, c * lanes : (c + 1) * lanes], half, 1) for c in range(3)], axis=1
        )
        straight = jnp.where(low_field, 0, 1) == which
        return jnp.where(straight, both, turned)

    seq[1] = term(0, 0)

    def advance(value, r):
        known = value + term((r + 1) // 2, (r + 1) % 2)
        seq[r + 2] = known + (0.5 * h) * coarse_finish(value, r + 2, c_acc.at[0])

    def open_stage(r):
        value = seq[r + 1]
        value3 = stacked(value)
        coarse_begin(value3, coarse_tab[1], r + 2)
        local(value, value3, coarse_tab, c_acc.at[0])
        return value

    def stage(r, carry):
        value = open_stage(r)
        source = (r + 1) // 2

        @pl.when((r % 2 == 1) & (source < p))
        def _():
            term_copy(source, 1).wait_recv()

        advance(value, r)
        return carry

    lax.fori_loop(0, 2 * p, stage, 0)
    value = open_stage(2 * p)

    @pl.when(p + 1 < slices)
    def _():
        hand_halo().start()

    @pl.when(p > 0)
    def _():
        hand_state().wait_recv()
        hand_halo().wait_recv()

    saved[5] = restrict(stacked(start[...]))

    wholes = ((start, saved.at[5]), (v1, saved.at[1]), (v2, saved.at[2]))

    def correct(m):
        whole, part = wholes[m]
        delta = seq[2 * p + m] - part[...]
        coarse_begin(stacked(delta), delta_faces, 2 * slices + 1 + m)
        nodes[m] = whole[...] + prolong(delta)

    for m in range(2):
        correct(m)
    advance(value, 2 * p)
    correct(2)
    for m in range(3):
        local(nodes[m], stacked(nodes[m]), fine_tab, f_acc.at[m])
    for m, base_halo in enumerate((start_halo, f_recv.at[1], f_recv.at[2])):
        got = arrive(coarse_part, 2 * slices + 1 + m)
        rates[m] = finish(nodes[m], fine_tab, base_halo[...] + prolong_halo(got), f_acc.at[m])

    for k in range(1, slices):
        @pl.when(p + k < slices)
        def _():
            term_copy(p, k).wait_send()

    @pl.when(p + 1 < slices)
    def _():
        hand_state().wait_send()
        hand_halo().wait_send()

    row = QUAD_WEIGHTS[0]
    v1[...] = nodes[0] + h * (row[0] * rates[0] + row[1] * rates[1] + row[2] * rates[2])
    value3 = stacked(v1[...])
    begin(value3, 3)
    local(v1[...], value3, fine_tab, f_acc.at[0])
    row = QUAD_WEIGHTS[1]
    v2[...] = v1[...] + h * (row[0] * rates[0] + (row[1] - 0.5) * rates[1] + row[2] * rates[2])
    last = v2[...] + (0.5 * h) * finish(v1[...], fine_tab, arrive(fine_part, 3), f_acc.at[0])
    for c in range(3):
        out_ref[c] = last[:, c * lanes : (c + 1) * lanes]


def solution(mesh):
    slices, bricks = mesh.shape["tm"], mesh.shape["space"]

    def shards(initial):
        side, z_length = initial.shape[3], initial.shape[-1]
        lanes = z_length
        half = side // 2
        fine_rows, coarse_rows = side * side, half * half
        fine_points, fine_weights = cheb_tables(FINE)
        coarse_points, coarse_weights = cheb_tables(COARSE)
        down = interp_matrix(fine_points, fine_weights, coarse_points)
        up = interp_matrix(coarse_points, coarse_weights, fine_points)
        spread = lambda m, length: np.kron(np.eye(length // m.shape[1]), m)
        down_side, up_side = spread(down, side), spread(up, half)
        fine_brick = lifted_matrix(FINE, side, False)
        slope_of = [fine_brick[:1] @ up_side, fine_brick[-1:] @ up_side]
        ident = np.eye(half)
        delta_slopes = [np.kron(m, ident) for m in slope_of] + [np.kron(ident, m) for m in slope_of]
        delta_values = face_rows(np.eye(half), half, True)[:4]
        spots = np.eye(8)
        halo_table = np.concatenate(
            [np.kron(spots[j : j + 1], up_side) for d in range(4) for j in (d, 4 + d)]
        )
        up_z = spread(up, z_length // 2).T
        down_z = spread(down, z_length).T
        tables = (
            level_tables(FINE, side, z_length, lanes, False)
            + level_tables(COARSE, half, z_length // 2, lanes, True)
            + [
                left_table(np.kron(down_side, down_side)),
                right_table(np.tile(down_z, (1, 2))),
                left_table(np.kron(up_side, up_side)),
                right_table(padded(up_z, lanes, lanes)),
                left_table(np.concatenate(delta_values + delta_slopes)),
                right_table(np.kron(np.eye(2), up_z)),
                left_table(halo_table),
            ]
        )
        wide = 3 * lanes
        tables = [padded(t, t.shape[0], -(-t.shape[1] // lanes) * lanes) for t in tables]
        banks, places = ([], []), []
        for t in tables:
            bank = int(t.shape[1] <= wide)
            places.append((bank, sum(len(other) for other in banks[bank])))
            width = wide if bank else tables[0].shape[1]
            banks[bank].append(padded(t, t.shape[0], width))
        banks = [np.concatenate(bank) for bank in banks]
        fine_slots, coarse_slots = 4, 2 * slices + 4
        fine_field = pltpu.VMEM((fine_rows, wide), F32)
        geometry = (slices, bricks, fine_rows, coarse_rows, lanes)
        result = pl.pallas_call(
            functools.partial(kernel, geometry, places),
            out_shape=jax.ShapeDtypeStruct((3, fine_rows, lanes), F32),
            in_specs=[pl.BlockSpec(memory_space=pl.ANY)] * 3,
            out_specs=pl.BlockSpec(memory_space=pltpu.VMEM),
            scratch_shapes=[pltpu.VMEM((3, fine_rows, lanes), F32)]
            + [pltpu.VMEM(t.shape, BF16) for t in tables]
            + [
                pltpu.SemaphoreType.DMA((len(tables) + 1,)),
                fine_field,
                fine_field,
                fine_field,
                pltpu.VMEM((8 * side, wide), F32),
                pltpu.VMEM((3, fine_rows, wide), F32),
                pltpu.VMEM((3, fine_rows, wide), F32),
                pltpu.VMEM((fine_slots, 8 * side, wide), F32),
                pltpu.VMEM((fine_slots, 8 * side, wide), F32),
                pltpu.VMEM((3, 3 * fine_rows, 2 * wide), F32),
                pltpu.VMEM((coarse_slots, 4 * half, wide), F32),
                pltpu.VMEM((coarse_slots, 4 * half, wide), F32),
                pltpu.VMEM((2, 3 * coarse_rows, 2 * wide), F32),
                pltpu.VMEM((2 * slices + 1, coarse_rows, wide), F32),
                pltpu.VMEM((slices, coarse_rows, wide), F32),
                pltpu.VMEM((6, coarse_rows, wide), F32),
                pltpu.SemaphoreType.DMA((fine_slots, 4)),
                pltpu.SemaphoreType.DMA((fine_slots, 4)),
                pltpu.SemaphoreType.DMA((coarse_slots, 4)),
                pltpu.SemaphoreType.DMA((coarse_slots, 4)),
                pltpu.SemaphoreType.DMA((slices,)),
                pltpu.SemaphoreType.DMA((slices,)),
                pltpu.SemaphoreType.DMA((2,)),
                pltpu.SemaphoreType.DMA((2,)),
            ],
            compiler_params=pltpu.CompilerParams(
                collective_id=0, has_side_effects=True, vmem_limit_bytes=VMEM_LIMIT
            ),
        )(initial.reshape(3, fine_rows, lanes), *[jnp.asarray(bank) for bank in banks])
        return result.reshape(initial.shape)

    return jax.shard_map(
        shards,
        mesh=mesh,
        in_specs=(P("tm", None, "space", None, None, None),),
        out_specs=P("tm", None, "space", None, None, None),
        check_vma=False,
    )
```

```python
import functools
import jax
import jax.numpy as jnp
import numpy as np
from jax import lax
from jax.experimental import pallas as pl
from jax.experimental.pallas import tpu as pltpu
from jax.sharding import PartitionSpec as P

YBRICKS = 4
FINE = 16
COARSE = 8
LANES = 128
TIME_STEP = 0.001
VISCOSITY = 0.05
QUAD_WEIGHTS = ((5.0 / 24.0, 1.0 / 3.0, -1.0 / 24.0), (-1.0 / 24.0, 1.0 / 3.0, 5.0 / 24.0))
MESH = pl.DeviceIdType.MESH
F32 = jnp.float32
BF16 = jnp.bfloat16
VMEM_LIMIT = 52 * 2**20
BANK_SPARE = 5504


def cheb_tables(count):
    index = np.arange(count)
    points = -np.cos(np.pi * index / (count - 1))
    weights = (-1.0) ** index
    weights[0] = weights[0] * 0.5
    weights[-1] = weights[-1] * 0.5
    return (points, weights)


def diff_matrix(points, weights):
    count = points.shape[0]
    ident = np.eye(count)
    gaps = points[:, None] - points[None, :] + ident
    matrix = weights[None, :] / weights[:, None] / gaps
    matrix = matrix * (1.0 - ident)
    return matrix - ident * matrix.sum(axis=1)[:, None]


def interp_matrix(points, weights, targets):
    gaps = targets[:, None] - points[None, :]
    exact_hit = np.abs(gaps) < 1e-12
    safe_gaps = np.where(exact_hit, 1.0, gaps)
    terms = weights[None, :] / safe_gaps
    matrix = terms / terms.sum(axis=1, keepdims=True)
    any_hit = exact_hit.any(axis=1)
    return np.where(any_hit[:, None], np.where(exact_hit, 1.0, 0.0), matrix)


def lifted_matrix(count, length, periodic):
    points, weights = cheb_tables(count)
    matrix = np.kron(np.eye(length // count), diff_matrix(points, weights))
    lift_coef = (count - 1) ** 2 / 2.0
    for place in range(length):
        if place % count == 0:
            matrix[place, place] += lift_coef
            if place > 0:
                matrix[place, place - 1] -= lift_coef
            elif periodic:
                matrix[place, length - 1] -= lift_coef
        if place % count == count - 1:
            matrix[place, place] -= lift_coef
            if place < length - 1:
                matrix[place, place + 1] += lift_coef
            elif periodic:
                matrix[place, 0] += lift_coef
    return matrix


def halves(matrix):
    high = np.asarray(matrix, np.float32).astype(jnp.bfloat16)
    low = (np.asarray(matrix, np.float64) - high.astype(np.float64)).astype(np.float32).astype(jnp.bfloat16)
    return high, low


def left_table(matrix):
    high, low = halves(matrix)
    return np.concatenate([high, high, low], axis=1)


def right_table(matrix):
    high, low = halves(matrix)
    return np.concatenate([high, high, low], axis=0)


def padded(matrix, rows, columns):
    return np.pad(matrix, ((0, rows - matrix.shape[0]), (0, columns - matrix.shape[1])))


def face_rows(brick, side, packed):
    ident = np.eye(side)
    ends = (ident[:1], ident[-1:])
    forms = (lambda m: np.kron(m, ident), lambda m: np.kron(ident, m))
    value = [form(e) for form in forms for e in ends]
    slope = [form(e @ brick) for form in forms for e in ends]
    if packed:
        return value + slope
    return [m for pair in zip(value, slope) for m in pair]


def level_tables(count, side, z_length, lanes, packed):
    brick = lifted_matrix(count, side, False)
    lift = (count - 1) ** 2 / 2.0
    ident = np.eye(side)
    first, last = ident[:, :1], ident[:, -1:]
    second = brick @ brick - lift**2 * (first @ first.T + last @ last.T)
    along_x = lambda m: np.kron(m, ident)
    along_y = lambda m: np.kron(ident, m)
    inner = np.concatenate(
        [along_x(brick), along_y(brick), VISCOSITY * (along_x(second) + along_y(second))]
    )
    faces = np.concatenate(face_rows(brick, side, packed))
    grad_cols, visc_cols = [], []
    for e, sign in ((first, -lift), (last, lift)):
        grad_cols += [sign * e, 0.0 * e]
        visc_cols += [VISCOSITY * sign * (brick @ e), VISCOSITY * sign * e]
    nothing = [0.0 * first] * 4
    order = [0, 2, 4, 6, 1, 3, 5, 7] if packed else list(range(8))

    def rows(cx, cy):
        columns = [along_x(m) for m in cx] + [along_y(m) for m in cy]
        return np.concatenate([columns[i] for i in order], axis=1)

    outer = np.concatenate(
        [rows(grad_cols, nothing), rows(nothing, grad_cols), rows(visc_cols, visc_cols)]
    )
    depth = lifted_matrix(count, z_length, True)
    twice = lanes // z_length
    depth_t = np.concatenate(
        [np.tile(m.T, (1, twice)) for m in (depth, VISCOSITY * (depth @ depth))], axis=1
    )
    depth_t = padded(depth_t, lanes, 2 * lanes)
    return [left_table(inner), left_table(faces), left_table(outer), right_table(depth_t)]


def split(value):
    high = value.astype(BF16)
    low = (value - high.astype(F32)).astype(BF16)
    return high, low


def stacked(value):
    high, low = split(value)
    return jnp.concatenate([high, low, high], axis=0)


def left(table, value3):
    return jnp.dot(table[:, : value3.shape[0]], value3, preferred_element_type=F32)


def right(value, table, lanes):
    high, low = split(value)
    blocks = []
    for at in range(0, value.shape[1], lanes):
        h, l = high[:, at : at + lanes], low[:, at : at + lanes]
        blocks.append(jnp.concatenate([h, l, h], axis=1))
    return jnp.dot(jnp.concatenate(blocks, axis=0), table[...], preferred_element_type=F32)


def unstack(value, rows):
    return jnp.concatenate([value[at : at + rows] for at in range(0, value.shape[0], rows)], axis=1)


def kernel(geometry, places, q_hbm, *refs):
    slices, bricks, fine_rows, coarse_rows, lanes = geometry
    table_count = len(places)
    bank, refs = refs[0], refs[1:]
    out_ref, q_ref, refs = refs[0], refs[1], refs[2:]
    tables, refs = refs[:table_count], refs[table_count:]
    fine_tab, coarse_tab = tables[:4], tables[4:8]
    (restrict_rows, restrict_z, prolong_rows, prolong_z,
     delta_faces, halo_z, halo_rows) = tables[8:]
    (l_sem, v1, v2, start, start_halo, rates, nodes, f_send, f_recv, f_acc, c_send, c_recv, c_acc,
     seq, terms, saved, f_ssem, f_rsem, c_ssem, c_rsem, t_ssem, t_rsem, s_ssem, s_rsem) = refs
    half = lanes // 2
    size = c_send.shape[1]

    q_load = pltpu.make_async_copy(q_hbm, q_ref, l_sem.at[table_count])
    q_load.start()
    loads = {}
    for i in (1, 0, 3, 2, 8, 9, 5, 4, 7, 6, 10, 11, 12, 13, 14):
        row, column = places[i]
        rows, columns = tables[i].shape
        loads[i] = pltpu.make_async_copy(
            bank.at[pl.ds(row, rows), pl.ds(column, columns)], tables[i], l_sem.at[i]
        )
        loads[i].start()

    p = lax.axis_index("tm")
    b = lax.axis_index("space")
    column = lax.rem(b, YBRICKS)
    base = b - column
    x_low = lax.rem(b + bricks - YBRICKS, bricks)
    x_high = lax.rem(b + YBRICKS, bricks)
    y_low = base + lax.rem(column + YBRICKS - 1, YBRICKS)
    y_high = base + lax.rem(column + 1, YBRICKS)
    targets = (x_low, x_high, y_low, y_high)
    landing = (1, 0, 3, 2)

    barrier = pltpu.get_barrier_semaphore()
    for target in targets:
        pl.semaphore_signal(barrier, inc=1, device_id={"space": target}, device_id_type=MESH)
    for k in range(1, slices):
        pl.semaphore_signal(
            barrier, inc=1, device_id={"tm": lax.rem(p + k, slices)}, device_id_type=MESH
        )
    pl.semaphore_wait(barrier, 4 + slices - 1)

    def face_copy(send, recv, ssem, rsem, slot, d, at, rows, which):
        size = send.shape[1] // 4
        return pltpu.make_async_remote_copy(
            src_ref=send.at[slot, pl.ds(d * size + at, rows)],
            dst_ref=recv.at[slot, pl.ds(landing[d] * size + at, rows)],
            send_sem=ssem.at[slot, 4 * which + d],
            recv_sem=rsem.at[slot, 4 * which + landing[d]],
            device_id={"space": targets[d]},
            device_id_type=MESH,
        )

    def copies(send, recv, ssem, rsem, slot):
        size = send.shape[1] // 4
        parts = (send, recv, ssem, rsem, slot)
        if send is not f_send:
            return [face_copy(*parts, d, 0, size, 0) for d in range(4)]
        return [face_copy(*parts, d, 0, size // 2, 0) for d in range(2)] + [
            face_copy(*parts, d, size // 2, size // 2, 1) for d in range(2)
        ] + [face_copy(*parts, d, 0, size, 0) for d in range(2, 4)]

    fine_part = (f_send, f_recv, f_ssem, f_rsem)
    coarse_part = (c_send, c_recv, c_ssem, c_rsem)
    low_lanes = lax.broadcasted_iota(jnp.int32, (size, 3 * lanes), 1) % lanes < half

    face = f_send.shape[1] // 8

    def begin(value, slot):
        parts = copies(*fine_part, slot)
        f_send[slot, :face] = value[:face]
        f_send[slot, 2 * face : 3 * face] = value[-face:]
        for copy in parts[:2]:
            copy.start()
        value3 = stacked(value)
        faces = left(fine_tab[1], value3)
        f_send[slot, face : 2 * face] = faces[face : 2 * face]
        f_send[slot, 3 * face :] = faces[3 * face :]
        for copy in parts[2:]:
            copy.start()
        return value3

    def coarse_begin(value3, table, slot):
        faces = left(table, value3)
        c_send[slot] = jnp.where(low_lanes, faces[:size], faces[size:])
        for copy in copies(*coarse_part, slot):
            copy.start()

    def arrive(part, slot):
        for copy in copies(*part, slot):
            copy.wait()
        return part[1][slot]

    def local(value, value3, tab, acc):
        rows = value.shape[0]
        acc[:, : 3 * lanes] = left(tab[0], value3)
        deep = right(value, tab[3], lanes)
        for c in range(3):
            at = slice(c * lanes, (c + 1) * lanes)
            one = deep[c * rows : (c + 1) * rows]
            acc[:rows, 3 * lanes + c * lanes : 4 * lanes + c * lanes] = one[:, :lanes]
            acc[2 * rows :, at] += one[:, lanes:]

    def finish(value, tab, halo, acc):
        rows = value.shape[0]
        total = acc[:, : 3 * lanes] + left(tab[2], stacked(halo))
        out = []
        for c in range(3):
            at = slice(c * lanes, (c + 1) * lanes)
            deep = acc[:rows, 3 * lanes + c * lanes : 4 * lanes + c * lanes]
            out.append(
                total[2 * rows :, at]
                - (
                    value[:, :lanes] * total[:rows, at]
                    + value[:, lanes : 2 * lanes] * total[rows : 2 * rows, at]
                    + value[:, 2 * lanes :] * deep
                )
            )
        return jnp.concatenate(out, axis=1)

    def coarse_finish(value, slot, acc):
        got = arrive(coarse_part, slot)
        turned = jnp.concatenate(
            [pltpu.roll(got[:, c * lanes : (c + 1) * lanes], half, 1) for c in range(3)], axis=1
        )
        halo = jnp.concatenate(
            [jnp.where(low_lanes, got, turned), jnp.where(low_lanes, turned, got)], axis=0
        )
        return finish(value, coarse_tab, halo, acc)

    def restrict(value3):
        return unstack(right(left(restrict_rows, value3), restrict_z, lanes), coarse_rows)

    def prolong(value):
        deep = unstack(right(value, prolong_z, lanes), coarse_rows)
        return left(prolong_rows, stacked(deep))

    def prolong_halo(got):
        both = right(got, halo_z, lanes)
        parts = [unstack(both[:, :lanes], size), unstack(both[:, lanes:], size)]
        return left(halo_rows, stacked(jnp.concatenate(parts, axis=0)))

    h = TIME_STEP
    q_load.wait()
    q = jnp.concatenate([q_ref[c] for c in range(3)], axis=1)
    loads[1].wait()
    value3 = begin(q, 0)
    for i in (0, 3):
        loads[i].wait()
    local(q, value3, fine_tab, f_acc.at[0])
    for i in (2, 8, 9):
        loads[i].wait()
    saved[0] = restrict(value3)
    seq[0] = saved[0]
    rates[0] = finish(q, fine_tab, arrive(fine_part, 0), f_acc.at[0])

    v1[...] = q + (0.5 * h) * rates[0]
    value3 = begin(v1[...], 1)
    saved[1] = restrict(value3)
    for i in (4, 5, 6, 7, 10, 11, 12, 13, 14):
        loads[i].wait()
    for m in range(2):
        coarse3 = stacked(saved[m])
        coarse_begin(coarse3, coarse_tab[1], m)
        local(saved[m], coarse3, coarse_tab, c_acc.at[m])
    local(v1[...], value3, fine_tab, f_acc.at[0])
    rates[1] = finish(v1[...], fine_tab, arrive(fine_part, 1), f_acc.at[0])
    v2[...] = v1[...] + (0.5 * h) * rates[1]
    value3 = begin(v2[...], 2)

    def hand_on(source, target, which):
        return pltpu.make_async_remote_copy(
            src_ref=source,
            dst_ref=target,
            send_sem=s_ssem.at[which],
            recv_sem=s_rsem.at[which],
            device_id={"tm": lax.rem(p + 1, slices)},
            device_id_type=MESH,
        )

    hand_state = lambda: hand_on(v2, start, 0)
    hand_halo = lambda: hand_on(f_recv.at[2], start_halo, 1)

    @pl.when(p + 1 < slices)
    def _():
        hand_state().start()

    @pl.when(p == 0)
    def _():
        for c in range(3):
            start[:, c * lanes : (c + 1) * lanes] = q_ref[c]
        start_halo[...] = f_recv[0]

    local(v2[...], value3, fine_tab, f_acc.at[0])
    for m in range(2):
        saved[3 + m] = coarse_finish(saved[m], m, c_acc.at[m])
    saved[2] = restrict(value3)
    known = [restrict(stacked(rates[0])), restrict(stacked(rates[1]))]
    known.append(restrict(stacked(finish(v2[...], fine_tab, arrive(fine_part, 2), f_acc.at[0]))))
    first, second = [
        h * (row[0] * known[0] + row[1] * known[1] + row[2] * known[2]) for row in QUAD_WEIGHTS
    ]
    first = first + jnp.where(p == 0, saved[0], (-0.5 * h) * saved[3])
    second = second - (0.5 * h) * saved[4]
    low_field = lax.broadcasted_iota(jnp.int32, first.shape, 1) % lanes < half
    terms[p] = jnp.where(low_field, first, second)

    def term_copy(source, k):
        return pltpu.make_async_remote_copy(
            src_ref=terms.at[source],
            dst_ref=terms.at[source],
            send_sem=t_ssem.at[k],
            recv_sem=t_rsem.at[source],
            device_id={"tm": lax.rem(p + k, slices)},
            device_id_type=MESH,
        )

    for k in range(slices - 1, 0, -1):
        @pl.when(p + k < slices)
        def _():
            term_copy(p, k).start()

    @pl.when(p > 0)
    def _():
        term_copy(0, 1).wait_recv()

    def term(source, which):
        both = terms[source]
        turned = jnp.concatenate(
            [pltpu.roll(both[:, c * lanes : (c + 1) * lanes], half, 1) for c in range(3)], axis=1
        )
        straight = jnp.where(low_field, 0, 1) == which
        return jnp.where(straight, both, turned)

    seq[1] = term(0, 0)

    def advance(value, r):
        known = value + term((r + 1) // 2, (r + 1) % 2)
        seq[r + 2] = known + (0.5 * h) * coarse_finish(value, r + 2, c_acc.at[0])

    def open_stage(r):
        value = seq[r + 1]
        value3 = stacked(value)
        coarse_begin(value3, coarse_tab[1], r + 2)
        local(value, value3, coarse_tab, c_acc.at[0])
        return value

    wholes = ((start, saved.at[5]), (v1, saved.at[1]), (v2, saved.at[2]))

    def correct(m):
        whole, part = wholes[m]
        delta = seq[2 * p + m] - part[...]
        coarse_begin(stacked(delta), delta_faces, 2 * slices + 1 + m)
        nodes[m] = whole[...] + prolong(delta)
        local(nodes[m], stacked(nodes[m]), fine_tab, f_acc.at[m])

    def stage(r, carry):
        value = open_stage(r)
        source = (r + 1) // 2

        @pl.when((r % 2 == 1) & (source < p))
        def _():
            term_copy(source, 1).wait_recv()

        @pl.when(r == 2 * p - 2)
        def _():
            hand_state().wait_recv()
            saved[5] = restrict(stacked(start[...]))

        @pl.when(r == 2 * p - 1)
        def _():
            correct(0)

        advance(value, r)
        return carry

    lax.fori_loop(0, 2 * p, stage, 0)
    value = open_stage(2 * p)

    @pl.when(p + 1 < slices)
    def _():
        hand_halo().start()

    @pl.when(p == 0)
    def _():
        saved[5] = restrict(stacked(start[...]))
        correct(0)

    correct(1)
    advance(value, 2 * p)
    correct(2)

    @pl.when(p > 0)
    def _():
        hand_halo().wait_recv()

    for m, base_halo in enumerate((start_halo, f_recv.at[1], f_recv.at[2])):
        got = arrive(coarse_part, 2 * slices + 1 + m)
        rates[m] = finish(nodes[m], fine_tab, base_halo[...] + prolong_halo(got), f_acc.at[m])

    for k in range(1, slices):
        @pl.when(p + k < slices)
        def _():
            term_copy(p, k).wait_send()

    @pl.when(p + 1 < slices)
    def _():
        hand_state().wait_send()
        hand_halo().wait_send()

    row = QUAD_WEIGHTS[0]
    v1[...] = nodes[0] + h * (row[0] * rates[0] + row[1] * rates[1] + row[2] * rates[2])
    value3 = begin(v1[...], 3)
    local(v1[...], value3, fine_tab, f_acc.at[0])
    row = QUAD_WEIGHTS[1]
    v2[...] = v1[...] + h * (row[0] * rates[0] + (row[1] - 0.5) * rates[1] + row[2] * rates[2])
    last = v2[...] + (0.5 * h) * finish(v1[...], fine_tab, arrive(fine_part, 3), f_acc.at[0])
    for c in range(3):
        out_ref[c] = last[:, c * lanes : (c + 1) * lanes]


def solution(mesh):
    slices, bricks = mesh.shape["tm"], mesh.shape["space"]

    def shards(initial):
        side, z_length = initial.shape[3], initial.shape[-1]
        lanes = z_length
        half = side // 2
        fine_rows, coarse_rows = side * side, half * half
        fine_points, fine_weights = cheb_tables(FINE)
        coarse_points, coarse_weights = cheb_tables(COARSE)
        down = interp_matrix(fine_points, fine_weights, coarse_points)
        up = interp_matrix(coarse_points, coarse_weights, fine_points)
        spread = lambda m, length: np.kron(np.eye(length // m.shape[1]), m)
        down_side, up_side = spread(down, side), spread(up, half)
        fine_brick = lifted_matrix(FINE, side, False)
        slope_of = [fine_brick[:1] @ up_side, fine_brick[-1:] @ up_side]
        ident = np.eye(half)
        delta_slopes = [np.kron(m, ident) for m in slope_of] + [np.kron(ident, m) for m in slope_of]
        delta_values = face_rows(np.eye(half), half, True)[:4]
        spots = np.eye(8)
        halo_table = np.concatenate(
            [np.kron(spots[j : j + 1], up_side) for d in range(4) for j in (d, 4 + d)]
        )
        up_z = spread(up, z_length // 2).T
        down_z = spread(down, z_length).T
        tables = (
            level_tables(FINE, side, z_length, lanes, False)
            + level_tables(COARSE, half, z_length // 2, lanes, True)
            + [
                left_table(np.kron(down_side, down_side)),
                right_table(np.tile(down_z, (1, 2))),
                left_table(np.kron(up_side, up_side)),
                right_table(padded(up_z, lanes, lanes)),
                left_table(np.concatenate(delta_values + delta_slopes)),
                right_table(np.kron(np.eye(2), up_z)),
                left_table(halo_table),
            ]
        )
        wide = 3 * lanes
        tables = [padded(t, t.shape[0], -(-t.shape[1] // lanes) * lanes) for t in tables]
        bank_width = 2 * wide
        places, heights = [], [0, 0]
        for t in sorted(range(len(tables)), key=lambda t: -tables[t].shape[1]):
            side_by = int(heights[1] < heights[0])
            places.append((t, heights[side_by], side_by * wide))
            for other in range(2) if tables[t].shape[1] > wide else (side_by,):
                heights[other] += tables[t].shape[0]
        places = [place[1:] for place in sorted(places)]
        bank = np.zeros((max(heights) + BANK_SPARE, bank_width), jnp.bfloat16)
        for t, (row, column) in zip(tables, places):
            bank[row : row + t.shape[0], column : column + t.shape[1]] = t
        fine_slots, coarse_slots = 4, 2 * slices + 4
        fine_field = pltpu.VMEM((fine_rows, wide), F32)
        geometry = (slices, bricks, fine_rows, coarse_rows, lanes)
        result = pl.pallas_call(
            functools.partial(kernel, geometry, places),
            out_shape=jax.ShapeDtypeStruct((3, fine_rows, lanes), F32),
            in_specs=[pl.BlockSpec(memory_space=pl.ANY)] * 2,
            out_specs=pl.BlockSpec(memory_space=pltpu.VMEM),
            scratch_shapes=[pltpu.VMEM((3, fine_rows, lanes), F32)]
            + [pltpu.VMEM(t.shape, BF16) for t in tables]
            + [
                pltpu.SemaphoreType.DMA((len(tables) + 1,)),
                fine_field,
                fine_field,
                fine_field,
                pltpu.VMEM((8 * side, wide), F32),
                pltpu.VMEM((3, fine_rows, wide), F32),
                pltpu.VMEM((3, fine_rows, wide), F32),
                pltpu.VMEM((fine_slots, 8 * side, wide), F32),
                pltpu.VMEM((fine_slots, 8 * side, wide), F32),
                pltpu.VMEM((3, 3 * fine_rows, 2 * wide), F32),
                pltpu.VMEM((coarse_slots, 4 * half, wide), F32),
                pltpu.VMEM((coarse_slots, 4 * half, wide), F32),
                pltpu.VMEM((2, 3 * coarse_rows, 2 * wide), F32),
                pltpu.VMEM((2 * slices + 1, coarse_rows, wide), F32),
                pltpu.VMEM((slices, coarse_rows, wide), F32),
                pltpu.VMEM((6, coarse_rows, wide), F32),
                pltpu.SemaphoreType.DMA((fine_slots, 8)),
                pltpu.SemaphoreType.DMA((fine_slots, 8)),
                pltpu.SemaphoreType.DMA((coarse_slots, 4)),
                pltpu.SemaphoreType.DMA((coarse_slots, 4)),
                pltpu.SemaphoreType.DMA((slices,)),
                pltpu.SemaphoreType.DMA((slices,)),
                pltpu.SemaphoreType.DMA((2,)),
                pltpu.SemaphoreType.DMA((2,)),
            ],
            compiler_params=pltpu.CompilerParams(
                collective_id=0, has_side_effects=True, vmem_limit_bytes=VMEM_LIMIT
            ),
        )(initial.reshape(3, fine_rows, lanes), jnp.asarray(bank))
        return result.reshape(initial.shape)

    return jax.shard_map(
        shards,
        mesh=mesh,
        in_specs=(P("tm", None, "space", None, None, None),),
        out_specs=P("tm", None, "space", None, None, None),
        check_vma=False,
    )
```

```python
import functools
import jax
import jax.numpy as jnp
import numpy as np
from jax import lax
from jax.experimental import pallas as pl
from jax.experimental.pallas import tpu as pltpu
from jax.sharding import PartitionSpec as P

YBRICKS = 4
FINE = 16
COARSE = 8
LANES = 128
TIME_STEP = 0.001
VISCOSITY = 0.05
QUAD_WEIGHTS = ((5.0 / 24.0, 1.0 / 3.0, -1.0 / 24.0), (-1.0 / 24.0, 1.0 / 3.0, 5.0 / 24.0))
MESH = pl.DeviceIdType.MESH
F32 = jnp.float32
BF16 = jnp.bfloat16
VMEM_LIMIT = 52 * 2**20
BANK_SPARE = 5504


def cheb_tables(count):
    index = np.arange(count)
    points = -np.cos(np.pi * index / (count - 1))
    weights = (-1.0) ** index
    weights[0] = weights[0] * 0.5
    weights[-1] = weights[-1] * 0.5
    return (points, weights)


def diff_matrix(points, weights):
    count = points.shape[0]
    ident = np.eye(count)
    gaps = points[:, None] - points[None, :] + ident
    matrix = weights[None, :] / weights[:, None] / gaps
    matrix = matrix * (1.0 - ident)
    return matrix - ident * matrix.sum(axis=1)[:, None]


def interp_matrix(points, weights, targets):
    gaps = targets[:, None] - points[None, :]
    exact_hit = np.abs(gaps) < 1e-12
    safe_gaps = np.where(exact_hit, 1.0, gaps)
    terms = weights[None, :] / safe_gaps
    matrix = terms / terms.sum(axis=1, keepdims=True)
    any_hit = exact_hit.any(axis=1)
    return np.where(any_hit[:, None], np.where(exact_hit, 1.0, 0.0), matrix)


def lifted_matrix(count, length, periodic):
    points, weights = cheb_tables(count)
    matrix = np.kron(np.eye(length // count), diff_matrix(points, weights))
    lift_coef = (count - 1) ** 2 / 2.0
    for place in range(length):
        if place % count == 0:
            matrix[place, place] += lift_coef
            if place > 0:
                matrix[place, place - 1] -= lift_coef
            elif periodic:
                matrix[place, length - 1] -= lift_coef
        if place % count == count - 1:
            matrix[place, place] -= lift_coef
            if place < length - 1:
                matrix[place, place + 1] += lift_coef
            elif periodic:
                matrix[place, 0] += lift_coef
    return matrix


def halves(matrix):
    high = np.asarray(matrix, np.float32).astype(jnp.bfloat16)
    low = (np.asarray(matrix, np.float64) - high.astype(np.float64)).astype(np.float32).astype(jnp.bfloat16)
    return high, low


def left_table(matrix):
    high, low = halves(matrix)
    return np.concatenate([high, high, low], axis=1)


def right_table(matrix):
    high, low = halves(matrix)
    return np.concatenate([high, high, low], axis=0)


def padded(matrix, rows, columns):
    return np.pad(matrix, ((0, rows - matrix.shape[0]), (0, columns - matrix.shape[1])))


def face_rows(brick, side, packed):
    ident = np.eye(side)
    ends = (ident[:1], ident[-1:])
    forms = (lambda m: np.kron(m, ident), lambda m: np.kron(ident, m))
    value = [form(e) for form in forms for e in ends]
    slope = [form(e @ brick) for form in forms for e in ends]
    if packed:
        return value + slope
    return [m for pair in zip(value, slope) for m in pair]


def level_tables(count, side, z_length, lanes, packed):
    brick = lifted_matrix(count, side, False)
    lift = (count - 1) ** 2 / 2.0
    ident = np.eye(side)
    first, last = ident[:, :1], ident[:, -1:]
    second = brick @ brick - lift**2 * (first @ first.T + last @ last.T)
    along_x = lambda m: np.kron(m, ident)
    along_y = lambda m: np.kron(ident, m)
    inner = np.concatenate(
        [along_x(brick), along_y(brick), VISCOSITY * (along_x(second) + along_y(second))]
    )
    faces = np.concatenate(face_rows(brick, side, packed))
    grad_cols, visc_cols = [], []
    for e, sign in ((first, -lift), (last, lift)):
        grad_cols += [sign * e, 0.0 * e]
        visc_cols += [VISCOSITY * sign * (brick @ e), VISCOSITY * sign * e]
    nothing = [0.0 * first] * 4
    order = [0, 2, 4, 6, 1, 3, 5, 7] if packed else list(range(8))

    def rows(cx, cy):
        columns = [along_x(m) for m in cx] + [along_y(m) for m in cy]
        return np.concatenate([columns[i] for i in order], axis=1)

    outer = np.concatenate(
        [rows(grad_cols, nothing), rows(nothing, grad_cols), rows(visc_cols, visc_cols)]
    )
    depth = lifted_matrix(count, z_length, True)
    twice = lanes // z_length
    depth_t = np.concatenate(
        [np.tile(m.T, (1, twice)) for m in (depth, VISCOSITY * (depth @ depth))], axis=1
    )
    depth_t = padded(depth_t, lanes, 2 * lanes)
    return [left_table(inner), left_table(faces), left_table(outer), right_table(depth_t)]


def split(value):
    high = value.astype(BF16)
    low = (value - high.astype(F32)).astype(BF16)
    return high, low


def stacked(value):
    high, low = split(value)
    return jnp.concatenate([high, low, high], axis=0)


def left(table, value3):
    return jnp.dot(table[:, : value3.shape[0]], value3, preferred_element_type=F32)


def right(value, table, lanes):
    high, low = split(value)
    blocks = []
    for at in range(0, value.shape[1], lanes):
        h, l = high[:, at : at + lanes], low[:, at : at + lanes]
        blocks.append(jnp.concatenate([h, l, h], axis=1))
    return jnp.dot(jnp.concatenate(blocks, axis=0), table[...], preferred_element_type=F32)


def unstack(value, rows):
    return jnp.concatenate([value[at : at + rows] for at in range(0, value.shape[0], rows)], axis=1)


def kernel(geometry, places, q_hbm, *refs):
    slices, bricks, fine_rows, coarse_rows, lanes = geometry
    table_count = len(places)
    bank, refs = refs[0], refs[1:]
    out_ref, q_ref, refs = refs[0], refs[1], refs[2:]
    tables, refs = refs[:table_count], refs[table_count:]
    fine_tab, coarse_tab = tables[:4], tables[4:8]
    (restrict_rows, restrict_z, prolong_rows, prolong_z,
     delta_faces, halo_z, halo_rows) = tables[8:]
    (l_sem, v1, v2, start, start_halo, rates, nodes, f_send, f_recv, f_acc, c_send, c_recv, c_acc,
     seq, terms, saved, f_ssem, f_rsem, c_ssem, c_rsem, t_ssem, t_rsem, s_ssem, s_rsem,
     chain, k_ssem, k_rsem) = refs
    half = lanes // 2
    size = c_send.shape[1]

    q_load = pltpu.make_async_copy(q_hbm, q_ref, l_sem.at[table_count])
    q_load.start()
    loads = {}
    for i in (1, 0, 3, 2, 8, 9, 5, 4, 7, 6, 10, 11, 12, 13, 14):
        row, column = places[i]
        rows, columns = tables[i].shape
        loads[i] = pltpu.make_async_copy(
            bank.at[pl.ds(row, rows), pl.ds(column, columns)], tables[i], l_sem.at[i]
        )
        loads[i].start()

    p = lax.axis_index("tm")
    b = lax.axis_index("space")
    column = lax.rem(b, YBRICKS)
    base = b - column
    x_low = lax.rem(b + bricks - YBRICKS, bricks)
    x_high = lax.rem(b + YBRICKS, bricks)
    y_low = base + lax.rem(column + YBRICKS - 1, YBRICKS)
    y_high = base + lax.rem(column + 1, YBRICKS)
    targets = (x_low, x_high, y_low, y_high)
    landing = (1, 0, 3, 2)

    barrier = pltpu.get_barrier_semaphore()
    for target in targets:
        pl.semaphore_signal(barrier, inc=1, device_id={"space": target}, device_id_type=MESH)
    for k in range(1, slices):
        pl.semaphore_signal(
            barrier, inc=1, device_id={"tm": lax.rem(p + k, slices)}, device_id_type=MESH
        )
    pl.semaphore_wait(barrier, 4 + slices - 1)

    def face_copy(send, recv, ssem, rsem, slot, d, at, rows, which):
        size = send.shape[1] // 4
        return pltpu.make_async_remote_copy(
            src_ref=send.at[slot, pl.ds(d * size + at, rows)],
            dst_ref=recv.at[slot, pl.ds(landing[d] * size + at, rows)],
            send_sem=ssem.at[slot, 4 * which + d],
            recv_sem=rsem.at[slot, 4 * which + landing[d]],
            device_id={"space": targets[d]},
            device_id_type=MESH,
        )

    def copies(send, recv, ssem, rsem, slot):
        size = send.shape[1] // 4
        parts = (send, recv, ssem, rsem, slot)
        if send is not f_send:
            return [face_copy(*parts, d, 0, size, 0) for d in range(4)]
        return [face_copy(*parts, d, 0, size // 2, 0) for d in range(2)] + [
            face_copy(*parts, d, size // 2, size // 2, 1) for d in range(2)
        ] + [face_copy(*parts, d, 0, size, 0) for d in range(2, 4)]

    fine_part = (f_send, f_recv, f_ssem, f_rsem)
    coarse_part = (c_send, c_recv, c_ssem, c_rsem)
    low_lanes = lax.broadcasted_iota(jnp.int32, (size, 3 * lanes), 1) % lanes < half

    face = f_send.shape[1] // 8

    def begin(value, slot):
        parts = copies(*fine_part, slot)
        f_send[slot, :face] = value[:face]
        f_send[slot, 2 * face : 3 * face] = value[-face:]
        for copy in parts[:2]:
            copy.start()
        value3 = stacked(value)
        faces = left(fine_tab[1], value3)
        f_send[slot, face : 2 * face] = faces[face : 2 * face]
        f_send[slot, 3 * face :] = faces[3 * face :]
        for copy in parts[2:]:
            copy.start()
        return value3

    def coarse_begin(value3, table, slot):
        faces = left(table, value3)
        c_send[slot] = jnp.where(low_lanes, faces[:size], faces[size:])
        for copy in copies(*coarse_part, slot):
            copy.start()

    def arrive(part, slot):
        for copy in copies(*part, slot):
            copy.wait()
        return part[1][slot]

    def local(value, value3, tab, acc):
        rows = value.shape[0]
        acc[:, : 3 * lanes] = left(tab[0], value3)
        deep = right(value, tab[3], lanes)
        for c in range(3):
            at = slice(c * lanes, (c + 1) * lanes)
            one = deep[c * rows : (c + 1) * rows]
            acc[:rows, 3 * lanes + c * lanes : 4 * lanes + c * lanes] = one[:, :lanes]
            acc[2 * rows :, at] += one[:, lanes:]

    def finish(value, tab, halo, acc):
        rows = value.shape[0]
        total = acc[:, : 3 * lanes] + left(tab[2], stacked(halo))
        out = []
        for c in range(3):
            at = slice(c * lanes, (c + 1) * lanes)
            deep = acc[:rows, 3 * lanes + c * lanes : 4 * lanes + c * lanes]
            out.append(
                total[2 * rows :, at]
                - (
                    value[:, :lanes] * total[:rows, at]
                    + value[:, lanes : 2 * lanes] * total[rows : 2 * rows, at]
                    + value[:, 2 * lanes :] * deep
                )
            )
        return jnp.concatenate(out, axis=1)

    def coarse_finish(value, slot, acc):
        got = arrive(coarse_part, slot)
        turned = jnp.concatenate(
            [pltpu.roll(got[:, c * lanes : (c + 1) * lanes], half, 1) for c in range(3)], axis=1
        )
        halo = jnp.concatenate(
            [jnp.where(low_lanes, got, turned), jnp.where(low_lanes, turned, got)], axis=0
        )
        return finish(value, coarse_tab, halo, acc)

    def restrict(value3):
        return unstack(right(left(restrict_rows, value3), restrict_z, lanes), coarse_rows)

    def prolong(value):
        deep = unstack(right(value, prolong_z, lanes), coarse_rows)
        return left(prolong_rows, stacked(deep))

    def prolong_halo(got):
        both = right(got, halo_z, lanes)
        parts = [unstack(both[:, :lanes], size), unstack(both[:, lanes:], size)]
        return left(halo_rows, stacked(jnp.concatenate(parts, axis=0)))

    h = TIME_STEP
    q_load.wait()
    q = jnp.concatenate([q_ref[c] for c in range(3)], axis=1)
    loads[1].wait()
    value3 = begin(q, 0)
    for i in (0, 3):
        loads[i].wait()
    local(q, value3, fine_tab, f_acc.at[0])
    for i in (2, 8, 9):
        loads[i].wait()
    saved[0] = restrict(value3)
    seq[0] = saved[0]
    rates[0] = finish(q, fine_tab, arrive(fine_part, 0), f_acc.at[0])

    v1[...] = q + (0.5 * h) * rates[0]
    value3 = begin(v1[...], 1)
    saved[1] = restrict(value3)
    for i in (4, 5, 6, 7, 10, 11, 12, 13, 14):
        loads[i].wait()
    for m in range(2):
        coarse3 = stacked(saved[m])
        coarse_begin(coarse3, coarse_tab[1], m)
        local(saved[m], coarse3, coarse_tab, c_acc.at[m])
    local(v1[...], value3, fine_tab, f_acc.at[0])
    rates[1] = finish(v1[...], fine_tab, arrive(fine_part, 1), f_acc.at[0])
    v2[...] = v1[...] + (0.5 * h) * rates[1]
    value3 = begin(v2[...], 2)

    def hand_on(source, target, which):
        return pltpu.make_async_remote_copy(
            src_ref=source,
            dst_ref=target,
            send_sem=s_ssem.at[which],
            recv_sem=s_rsem.at[which],
            device_id={"tm": lax.rem(p + 1, slices)},
            device_id_type=MESH,
        )

    hand_state = lambda: hand_on(v2, start, 0)
    hand_halo = lambda: hand_on(f_recv.at[2], start_halo, 1)

    @pl.when(p + 1 < slices)
    def _():
        hand_state().start()

    @pl.when(p == 0)
    def _():
        for c in range(3):
            start[:, c * lanes : (c + 1) * lanes] = q_ref[c]
        start_halo[...] = f_recv[0]

    local(v2[...], value3, fine_tab, f_acc.at[0])
    for m in range(2):
        saved[3 + m] = coarse_finish(saved[m], m, c_acc.at[m])
    saved[2] = restrict(value3)
    known = [restrict(stacked(rates[0])), restrict(stacked(rates[1]))]
    known.append(restrict(stacked(finish(v2[...], fine_tab, arrive(fine_part, 2), f_acc.at[0]))))
    first, second = [
        h * (row[0] * known[0] + row[1] * known[1] + row[2] * known[2]) for row in QUAD_WEIGHTS
    ]
    first = first + jnp.where(p == 0, saved[0], (-0.5 * h) * saved[3])
    second = second - (0.5 * h) * saved[4]
    low_field = lax.broadcasted_iota(jnp.int32, first.shape, 1) % lanes < half
    terms[p] = jnp.where(low_field, first, second)

    def term_copy(source, k):
        return pltpu.make_async_remote_copy(
            src_ref=terms.at[source],
            dst_ref=terms.at[source],
            send_sem=t_ssem.at[k],
            recv_sem=t_rsem.at[source],
            device_id={"tm": lax.rem(p + k, slices)},
            device_id_type=MESH,
        )

    low_chain = low_field[: coarse_rows // 2]
    odd = lax.rem(p, 2)
    chip = p - odd
    sends_term = (odd == 0) & (p + 1 < slices)

    @pl.when(sends_term)
    def _():
        term_copy(p, 1).start()

    @pl.when(odd == 1)
    def _():
        term_copy(p - 1, 1).wait_recv()

    def chain_copy(k):
        return pltpu.make_async_remote_copy(
            src_ref=chain.at[0],
            dst_ref=chain.at[1],
            send_sem=k_ssem.at[k - 1],
            recv_sem=k_rsem,
            device_id={"tm": lax.rem(p + k, slices)},
            device_id_type=MESH,
        )

    def take_start():
        hand_state().wait_recv()
        saved[5] = restrict(stacked(start[...]))

    def term(source, which):
        both = terms[source]
        turned = jnp.concatenate(
            [pltpu.roll(both[:, c * lanes : (c + 1) * lanes], half, 1) for c in range(3)], axis=1
        )
        straight = jnp.where(low_field, 0, 1) == which
        return jnp.where(straight, both, turned)

    @pl.when(chip == 0)
    def _():
        seq[1] = term(0, 0)

    @pl.when(chip > 0)
    def _():
        take_start()
        chain_copy(1).wait_recv()
        both = chain[1]
        turned = jnp.concatenate(
            [pltpu.roll(both[:, c * lanes : (c + 1) * lanes], half, 1) for c in range(3)], axis=1
        )
        seq[2 * chip, : coarse_rows // 2] = jnp.where(low_chain, both, turned)
        seq[2 * chip, coarse_rows // 2 :] = jnp.where(low_chain, turned, both)

    def advance(value, r):
        known = value + term((r + 1) // 2, (r + 1) % 2)
        seq[r + 2] = known + (0.5 * h) * coarse_finish(value, r + 2, c_acc.at[0])

    def open_stage(r):
        value = seq[r + 1]
        value3 = stacked(value)
        coarse_begin(value3, coarse_tab[1], r + 2)
        local(value, value3, coarse_tab, c_acc.at[0])
        return value

    wholes = ((start, saved.at[5]), (v1, saved.at[1]), (v2, saved.at[2]))

    def correct(m):
        whole, part = wholes[m]
        delta = seq[2 * p + m] - part[...]
        coarse_begin(stacked(delta), delta_faces, 2 * slices + 1 + m)
        nodes[m] = whole[...] + prolong(delta)
        local(nodes[m], stacked(nodes[m]), fine_tab, f_acc.at[m])

    def stage(r, carry):
        value = open_stage(r)

        @pl.when((chip == 0) & (r == 0))
        def _():
            take_start()

        @pl.when(r == 2 * p - 1)
        def _():
            correct(0)

        advance(value, r)
        return carry

    lax.fori_loop(jnp.maximum(2 * chip - 1, 0), 2 * p, stage, 0)
    value = open_stage(2 * p)

    @pl.when(p + 1 < slices)
    def _():
        hand_halo().start()

    @pl.when(p == 0)
    def _():
        saved[5] = restrict(stacked(start[...]))
        correct(0)

    correct(1)
    advance(value, 2 * p)
    chain_on = [(odd == 1) & (p + k < slices) for k in (1, 2)]

    @pl.when(chain_on[0])
    def _():
        node = seq[2 * p + 2]
        chain[0] = jnp.where(low_chain, node[: coarse_rows // 2], node[coarse_rows // 2 :])

    for k in (2, 1):
        @pl.when(chain_on[k - 1])
        def _():
            chain_copy(k).start()

    correct(2)

    @pl.when(p > 0)
    def _():
        hand_halo().wait_recv()

    for m, base_halo in enumerate((start_halo, f_recv.at[1], f_recv.at[2])):
        got = arrive(coarse_part, 2 * slices + 1 + m)
        rates[m] = finish(nodes[m], fine_tab, base_halo[...] + prolong_halo(got), f_acc.at[m])

    @pl.when(sends_term)
    def _():
        term_copy(p, 1).wait_send()

    for k in (2, 1):
        @pl.when(chain_on[k - 1])
        def _():
            chain_copy(k).wait_send()

    @pl.when(p + 1 < slices)
    def _():
        hand_state().wait_send()
        hand_halo().wait_send()

    row = QUAD_WEIGHTS[0]
    v1[...] = nodes[0] + h * (row[0] * rates[0] + row[1] * rates[1] + row[2] * rates[2])
    value3 = begin(v1[...], 3)
    local(v1[...], value3, fine_tab, f_acc.at[0])
    row = QUAD_WEIGHTS[1]
    v2[...] = v1[...] + h * (row[0] * rates[0] + (row[1] - 0.5) * rates[1] + row[2] * rates[2])
    last = v2[...] + (0.5 * h) * finish(v1[...], fine_tab, arrive(fine_part, 3), f_acc.at[0])
    for c in range(3):
        out_ref[c] = last[:, c * lanes : (c + 1) * lanes]


def solution(mesh):
    slices, bricks = mesh.shape["tm"], mesh.shape["space"]

    def shards(initial):
        side, z_length = initial.shape[3], initial.shape[-1]
        lanes = z_length
        half = side // 2
        fine_rows, coarse_rows = side * side, half * half
        fine_points, fine_weights = cheb_tables(FINE)
        coarse_points, coarse_weights = cheb_tables(COARSE)
        down = interp_matrix(fine_points, fine_weights, coarse_points)
        up = interp_matrix(coarse_points, coarse_weights, fine_points)
        spread = lambda m, length: np.kron(np.eye(length // m.shape[1]), m)
        down_side, up_side = spread(down, side), spread(up, half)
        fine_brick = lifted_matrix(FINE, side, False)
        slope_of = [fine_brick[:1] @ up_side, fine_brick[-1:] @ up_side]
        ident = np.eye(half)
        delta_slopes = [np.kron(m, ident) for m in slope_of] + [np.kron(ident, m) for m in slope_of]
        delta_values = face_rows(np.eye(half), half, True)[:4]
        spots = np.eye(8)
        halo_table = np.concatenate(
            [np.kron(spots[j : j + 1], up_side) for d in range(4) for j in (d, 4 + d)]
        )
        up_z = spread(up, z_length // 2).T
        down_z = spread(down, z_length).T
        tables = (
            level_tables(FINE, side, z_length, lanes, False)
            + level_tables(COARSE, half, z_length // 2, lanes, True)
            + [
                left_table(np.kron(down_side, down_side)),
                right_table(np.tile(down_z, (1, 2))),
                left_table(np.kron(up_side, up_side)),
                right_table(padded(up_z, lanes, lanes)),
                left_table(np.concatenate(delta_values + delta_slopes)),
                right_table(np.kron(np.eye(2), up_z)),
                left_table(halo_table),
            ]
        )
        wide = 3 * lanes
        tables = [padded(t, t.shape[0], -(-t.shape[1] // lanes) * lanes) for t in tables]
        bank_width = 2 * wide
        places, heights = [], [0, 0]
        for t in sorted(range(len(tables)), key=lambda t: -tables[t].shape[1]):
            side_by = int(heights[1] < heights[0])
            places.append((t, heights[side_by], side_by * wide))
            for other in range(2) if tables[t].shape[1] > wide else (side_by,):
                heights[other] += tables[t].shape[0]
        places = [place[1:] for place in sorted(places)]
        bank = np.zeros((max(heights) + BANK_SPARE, bank_width), jnp.bfloat16)
        for t, (row, column) in zip(tables, places):
            bank[row : row + t.shape[0], column : column + t.shape[1]] = t
        fine_slots, coarse_slots = 4, 2 * slices + 4
        fine_field = pltpu.VMEM((fine_rows, wide), F32)
        geometry = (slices, bricks, fine_rows, coarse_rows, lanes)
        result = pl.pallas_call(
            functools.partial(kernel, geometry, places),
            out_shape=jax.ShapeDtypeStruct((3, fine_rows, lanes), F32),
            in_specs=[pl.BlockSpec(memory_space=pl.ANY)] * 2,
            out_specs=pl.BlockSpec(memory_space=pltpu.VMEM),
            scratch_shapes=[pltpu.VMEM((3, fine_rows, lanes), F32)]
            + [pltpu.VMEM(t.shape, BF16) for t in tables]
            + [
                pltpu.SemaphoreType.DMA((len(tables) + 1,)),
                fine_field,
                fine_field,
                fine_field,
                pltpu.VMEM((8 * side, wide), F32),
                pltpu.VMEM((3, fine_rows, wide), F32),
                pltpu.VMEM((3, fine_rows, wide), F32),
                pltpu.VMEM((fine_slots, 8 * side, wide), F32),
                pltpu.VMEM((fine_slots, 8 * side, wide), F32),
                pltpu.VMEM((3, 3 * fine_rows, 2 * wide), F32),
                pltpu.VMEM((coarse_slots, 4 * half, wide), F32),
                pltpu.VMEM((coarse_slots, 4 * half, wide), F32),
                pltpu.VMEM((2, 3 * coarse_rows, 2 * wide), F32),
                pltpu.VMEM((2 * slices + 1, coarse_rows, wide), F32),
                pltpu.VMEM((slices, coarse_rows, wide), F32),
                pltpu.VMEM((6, coarse_rows, wide), F32),
                pltpu.SemaphoreType.DMA((fine_slots, 8)),
                pltpu.SemaphoreType.DMA((fine_slots, 8)),
                pltpu.SemaphoreType.DMA((coarse_slots, 4)),
                pltpu.SemaphoreType.DMA((coarse_slots, 4)),
                pltpu.SemaphoreType.DMA((slices,)),
                pltpu.SemaphoreType.DMA((slices,)),
                pltpu.SemaphoreType.DMA((2,)),
                pltpu.SemaphoreType.DMA((2,)),
                pltpu.VMEM((2, coarse_rows // 2, wide), F32),
                pltpu.SemaphoreType.DMA((2,)),
                pltpu.SemaphoreType.DMA,
            ],
            compiler_params=pltpu.CompilerParams(
                collective_id=0, has_side_effects=True, vmem_limit_bytes=VMEM_LIMIT
            ),
        )(initial.reshape(3, fine_rows, lanes), jnp.asarray(bank))
        return result.reshape(initial.shape)

    return jax.shard_map(
        shards,
        mesh=mesh,
        in_specs=(P("tm", None, "space", None, None, None),),
        out_specs=P("tm", None, "space", None, None, None),
        check_vma=False,
    )
```

```python
import functools
import jax
import jax.numpy as jnp
import numpy as np
from jax import lax
from jax.experimental import pallas as pl
from jax.experimental.pallas import tpu as pltpu
from jax.sharding import PartitionSpec as P

YBRICKS = 4
FINE = 16
COARSE = 8
LANES = 128
TIME_STEP = 0.001
VISCOSITY = 0.05
QUAD_WEIGHTS = ((5.0 / 24.0, 1.0 / 3.0, -1.0 / 24.0), (-1.0 / 24.0, 1.0 / 3.0, 5.0 / 24.0))
MESH = pl.DeviceIdType.MESH
F32 = jnp.float32
BF16 = jnp.bfloat16
VMEM_LIMIT = 52 * 2**20
BANK_SPARE = 5504


def cheb_tables(count):
    index = np.arange(count)
    points = -np.cos(np.pi * index / (count - 1))
    weights = (-1.0) ** index
    weights[0] = weights[0] * 0.5
    weights[-1] = weights[-1] * 0.5
    return (points, weights)


def diff_matrix(points, weights):
    count = points.shape[0]
    ident = np.eye(count)
    gaps = points[:, None] - points[None, :] + ident
    matrix = weights[None, :] / weights[:, None] / gaps
    matrix = matrix * (1.0 - ident)
    return matrix - ident * matrix.sum(axis=1)[:, None]


def interp_matrix(points, weights, targets):
    gaps = targets[:, None] - points[None, :]
    exact_hit = np.abs(gaps) < 1e-12
    safe_gaps = np.where(exact_hit, 1.0, gaps)
    terms = weights[None, :] / safe_gaps
    matrix = terms / terms.sum(axis=1, keepdims=True)
    any_hit = exact_hit.any(axis=1)
    return np.where(any_hit[:, None], np.where(exact_hit, 1.0, 0.0), matrix)


def lifted_matrix(count, length, periodic):
    points, weights = cheb_tables(count)
    matrix = np.kron(np.eye(length // count), diff_matrix(points, weights))
    lift_coef = (count - 1) ** 2 / 2.0
    for place in range(length):
        if place % count == 0:
            matrix[place, place] += lift_coef
            if place > 0:
                matrix[place, place - 1] -= lift_coef
            elif periodic:
                matrix[place, length - 1] -= lift_coef
        if place % count == count - 1:
            matrix[place, place] -= lift_coef
            if place < length - 1:
                matrix[place, place + 1] += lift_coef
            elif periodic:
                matrix[place, 0] += lift_coef
    return matrix


def halves(matrix):
    high = np.asarray(matrix, np.float32).astype(jnp.bfloat16)
    low = (np.asarray(matrix, np.float64) - high.astype(np.float64)).astype(np.float32).astype(jnp.bfloat16)
    return high, low


def left_table(matrix):
    high, low = halves(matrix)
    return np.concatenate([high, high, low], axis=1)


def right_table(matrix):
    high, low = halves(matrix)
    return np.concatenate([high, high, low], axis=0)


def padded(matrix, rows, columns):
    return np.pad(matrix, ((0, rows - matrix.shape[0]), (0, columns - matrix.shape[1])))


def face_rows(brick, side, packed):
    ident = np.eye(side)
    ends = (ident[:1], ident[-1:])
    forms = (lambda m: np.kron(m, ident), lambda m: np.kron(ident, m))
    value = [form(e) for form in forms for e in ends]
    slope = [form(e @ brick) for form in forms for e in ends]
    if packed:
        return value + slope
    return [m for pair in zip(value, slope) for m in pair]


def level_tables(count, side, z_length, lanes, packed):
    brick = lifted_matrix(count, side, False)
    lift = (count - 1) ** 2 / 2.0
    ident = np.eye(side)
    first, last = ident[:, :1], ident[:, -1:]
    second = brick @ brick - lift**2 * (first @ first.T + last @ last.T)
    along_x = lambda m: np.kron(m, ident)
    along_y = lambda m: np.kron(ident, m)
    inner = np.concatenate(
        [along_x(brick), along_y(brick), VISCOSITY * (along_x(second) + along_y(second))]
    )
    faces = np.concatenate(face_rows(brick, side, packed))
    grad_cols, visc_cols = [], []
    for e, sign in ((first, -lift), (last, lift)):
        grad_cols += [sign * e, 0.0 * e]
        visc_cols += [VISCOSITY * sign * (brick @ e), VISCOSITY * sign * e]
    nothing = [0.0 * first] * 4
    order = [0, 2, 4, 6, 1, 3, 5, 7] if packed else list(range(8))

    def rows(cx, cy):
        columns = [along_x(m) for m in cx] + [along_y(m) for m in cy]
        return np.concatenate([columns[i] for i in order], axis=1)

    outer = np.concatenate(
        [rows(grad_cols, nothing), rows(nothing, grad_cols), rows(visc_cols, visc_cols)]
    )
    depth = lifted_matrix(count, z_length, True)
    twice = lanes // z_length
    depth_t = np.concatenate(
        [np.tile(m.T, (1, twice)) for m in (depth, VISCOSITY * (depth @ depth))], axis=1
    )
    depth_t = padded(depth_t, lanes, 2 * lanes)
    return [left_table(inner), left_table(faces), left_table(outer), right_table(depth_t)]


def split(value):
    high = value.astype(BF16)
    low = (value - high.astype(F32)).astype(BF16)
    return high, low


def stacked(value):
    high, low = split(value)
    return jnp.concatenate([high, low, high], axis=0)


def left(table, value3):
    return jnp.dot(table[:, : value3.shape[0]], value3, preferred_element_type=F32)


def right(value, table, lanes):
    high, low = split(value)
    blocks = []
    for at in range(0, value.shape[1], lanes):
        h, l = high[:, at : at + lanes], low[:, at : at + lanes]
        blocks.append(jnp.concatenate([h, l, h], axis=1))
    return jnp.dot(jnp.concatenate(blocks, axis=0), table[...], preferred_element_type=F32)


def unstack(value, rows):
    return jnp.concatenate([value[at : at + rows] for at in range(0, value.shape[0], rows)], axis=1)


def kernel(geometry, places, q_hbm, *refs):
    slices, bricks, fine_rows, coarse_rows, lanes = geometry
    table_count = len(places)
    bank, refs = refs[0], refs[1:]
    out_ref, q_ref, refs = refs[0], refs[1], refs[2:]
    tables, refs = refs[:table_count], refs[table_count:]
    fine_tab, coarse_tab = tables[:4], tables[4:8]
    (restrict_rows, restrict_z, prolong_rows, prolong_z,
     delta_faces, halo_z, halo_rows) = tables[8:]
    (l_sem, v1, v2, start, start_halo, rates, nodes, f_send, f_recv, f_acc, c_send, c_recv, c_acc,
     seq, terms, saved, f_ssem, f_rsem, c_ssem, c_rsem, t_ssem, t_rsem, s_ssem, s_rsem,
     chain, k_ssem, k_rsem) = refs
    half = lanes // 2
    size = c_send.shape[1]

    q_load = pltpu.make_async_copy(q_hbm, q_ref, l_sem.at[table_count])
    q_load.start()
    loads = {}
    for i in (1, 0, 3, 2, 8, 9, 5, 4, 7, 6, 10, 11, 12, 13, 14):
        row, column = places[i]
        rows, columns = tables[i].shape
        loads[i] = pltpu.make_async_copy(
            bank.at[pl.ds(row, rows), pl.ds(column, columns)], tables[i], l_sem.at[i]
        )
        loads[i].start()

    p = lax.axis_index("tm")
    b = lax.axis_index("space")
    column = lax.rem(b, YBRICKS)
    base = b - column
    x_low = lax.rem(b + bricks - YBRICKS, bricks)
    x_high = lax.rem(b + YBRICKS, bricks)
    y_low = base + lax.rem(column + YBRICKS - 1, YBRICKS)
    y_high = base + lax.rem(column + 1, YBRICKS)
    targets = (x_low, x_high, y_low, y_high)
    landing = (1, 0, 3, 2)

    barrier = pltpu.get_barrier_semaphore()
    for target in targets:
        pl.semaphore_signal(barrier, inc=1, device_id={"space": target}, device_id_type=MESH)
    for k in range(1, slices):
        pl.semaphore_signal(
            barrier, inc=1, device_id={"tm": lax.rem(p + k, slices)}, device_id_type=MESH
        )
    pl.semaphore_wait(barrier, 4 + slices - 1)

    def face_copy(send, recv, ssem, rsem, slot, d, at, rows, which):
        size = send.shape[1] // 4
        return pltpu.make_async_remote_copy(
            src_ref=send.at[slot, pl.ds(d * size + at, rows)],
            dst_ref=recv.at[slot, pl.ds(landing[d] * size + at, rows)],
            send_sem=ssem.at[slot, 4 * which + d],
            recv_sem=rsem.at[slot, 4 * which + landing[d]],
            device_id={"space": targets[d]},
            device_id_type=MESH,
        )

    def copies(send, recv, ssem, rsem, slot):
        size = send.shape[1] // 4
        parts = (send, recv, ssem, rsem, slot)
        if send is not f_send:
            return [face_copy(*parts, d, 0, size, 0) for d in range(4)]
        return [face_copy(*parts, d, 0, size // 2, 0) for d in range(2)] + [
            face_copy(*parts, d, size // 2, size // 2, 1) for d in range(2)
        ] + [face_copy(*parts, d, 0, size, 0) for d in range(2, 4)]

    fine_part = (f_send, f_recv, f_ssem, f_rsem)
    coarse_part = (c_send, c_recv, c_ssem, c_rsem)
    low_lanes = lax.broadcasted_iota(jnp.int32, (size, 3 * lanes), 1) % lanes < half

    face = f_send.shape[1] // 8

    def begin(value, slot):
        parts = copies(*fine_part, slot)
        f_send[slot, :face] = value[:face]
        f_send[slot, 2 * face : 3 * face] = value[-face:]
        for copy in parts[:2]:
            copy.start()
        value3 = stacked(value)
        faces = left(fine_tab[1], value3)
        f_send[slot, face : 2 * face] = faces[face : 2 * face]
        f_send[slot, 3 * face :] = faces[3 * face :]
        for copy in parts[2:]:
            copy.start()
        return value3

    def coarse_begin(value3, table, slot):
        faces = left(table, value3)
        c_send[slot] = jnp.where(low_lanes, faces[:size], faces[size:])
        for copy in copies(*coarse_part, slot):
            copy.start()

    def arrive(part, slot):
        for copy in copies(*part, slot):
            copy.wait()
        return part[1][slot]

    def local(value, value3, tab, acc):
        rows = value.shape[0]
        acc[:, : 3 * lanes] = left(tab[0], value3)
        deep = right(value, tab[3], lanes)
        for c in range(3):
            at = slice(c * lanes, (c + 1) * lanes)
            one = deep[c * rows : (c + 1) * rows]
            acc[:rows, 3 * lanes + c * lanes : 4 * lanes + c * lanes] = one[:, :lanes]
            acc[2 * rows :, at] += one[:, lanes:]

    def finish(value, tab, halo, acc):
        rows = value.shape[0]
        total = acc[:, : 3 * lanes] + left(tab[2], stacked(halo))
        out = []
        for c in range(3):
            at = slice(c * lanes, (c + 1) * lanes)
            deep = acc[:rows, 3 * lanes + c * lanes : 4 * lanes + c * lanes]
            out.append(
                total[2 * rows :, at]
                - (
                    value[:, :lanes] * total[:rows, at]
                    + value[:, lanes : 2 * lanes] * total[rows : 2 * rows, at]
                    + value[:, 2 * lanes :] * deep
                )
            )
        return jnp.concatenate(out, axis=1)

    def coarse_finish(value, slot, acc):
        got = arrive(coarse_part, slot)
        turned = jnp.concatenate(
            [pltpu.roll(got[:, c * lanes : (c + 1) * lanes], half, 1) for c in range(3)], axis=1
        )
        halo = jnp.concatenate(
            [jnp.where(low_lanes, got, turned), jnp.where(low_lanes, turned, got)], axis=0
        )
        return finish(value, coarse_tab, halo, acc)

    def restrict(value3):
        return unstack(right(left(restrict_rows, value3), restrict_z, lanes), coarse_rows)

    def prolong(value):
        deep = unstack(right(value, prolong_z, lanes), coarse_rows)
        return left(prolong_rows, stacked(deep))

    def prolong_halo(got):
        both = right(got, halo_z, lanes)
        parts = [unstack(both[:, :lanes], size), unstack(both[:, lanes:], size)]
        return left(halo_rows, stacked(jnp.concatenate(parts, axis=0)))

    h = TIME_STEP
    q_load.wait()
    q = jnp.concatenate([q_ref[c] for c in range(3)], axis=1)
    loads[1].wait()
    value3 = begin(q, 0)
    for i in (0, 3):
        loads[i].wait()
    local(q, value3, fine_tab, f_acc.at[0])
    for i in (2, 8, 9):
        loads[i].wait()
    saved[0] = restrict(value3)
    seq[0] = saved[0]
    rates[0] = finish(q, fine_tab, arrive(fine_part, 0), f_acc.at[0])

    v1[...] = q + (0.5 * h) * rates[0]
    value3 = begin(v1[...], 1)
    saved[1] = restrict(value3)
    for i in (4, 5, 6, 7, 10, 11, 12, 13, 14):
        loads[i].wait()
    for m in range(2):
        coarse3 = stacked(saved[m])
        coarse_begin(coarse3, coarse_tab[1], m)
        local(saved[m], coarse3, coarse_tab, c_acc.at[m])
    local(v1[...], value3, fine_tab, f_acc.at[0])
    rates[1] = finish(v1[...], fine_tab, arrive(fine_part, 1), f_acc.at[0])
    v2[...] = v1[...] + (0.5 * h) * rates[1]
    value3 = begin(v2[...], 2)

    def hand_on(source, target, which):
        return pltpu.make_async_remote_copy(
            src_ref=source,
            dst_ref=target,
            send_sem=s_ssem.at[which],
            recv_sem=s_rsem.at[which],
            device_id={"tm": lax.rem(p + 1, slices)},
            device_id_type=MESH,
        )

    hand_state = lambda: hand_on(v2, start, 0)
    hand_halo = lambda: hand_on(f_recv.at[2], start_halo, 1)

    @pl.when(p + 1 < slices)
    def _():
        hand_state().start()

    @pl.when(p == 0)
    def _():
        for c in range(3):
            start[:, c * lanes : (c + 1) * lanes] = q_ref[c]
        start_halo[...] = f_recv[0]

    local(v2[...], value3, fine_tab, f_acc.at[0])
    for m in range(2):
        saved[3 + m] = coarse_finish(saved[m], m, c_acc.at[m])
    saved[2] = restrict(value3)
    known = [restrict(stacked(rates[0])), restrict(stacked(rates[1]))]
    known.append(restrict(stacked(finish(v2[...], fine_tab, arrive(fine_part, 2), f_acc.at[0]))))
    first, second = [
        h * (row[0] * known[0] + row[1] * known[1] + row[2] * known[2]) for row in QUAD_WEIGHTS
    ]
    first = first + jnp.where(p == 0, saved[0], (-0.5 * h) * saved[3])
    second = second - (0.5 * h) * saved[4]
    low_field = lax.broadcasted_iota(jnp.int32, first.shape, 1) % lanes < half
    terms[p] = jnp.where(low_field, first, second)

    def term_copy(source, k):
        return pltpu.make_async_remote_copy(
            src_ref=terms.at[source],
            dst_ref=terms.at[source],
            send_sem=t_ssem.at[k],
            recv_sem=t_rsem.at[source],
            device_id={"tm": lax.rem(p + k, slices)},
            device_id_type=MESH,
        )

    low_chain = low_field[: coarse_rows // 2]
    odd = lax.rem(p, 2)
    chip = p - odd
    sends_term = (odd == 0) & (p + 1 < slices)

    @pl.when(sends_term)
    def _():
        term_copy(p, 1).start()

    @pl.when(p + 1 < slices)
    def _():
        hand_halo().start()

    @pl.when(odd == 1)
    def _():
        term_copy(p - 1, 1).wait_recv()

    def chain_copy(k):
        return pltpu.make_async_remote_copy(
            src_ref=chain.at[0],
            dst_ref=chain.at[1],
            send_sem=k_ssem.at[k - 1],
            recv_sem=k_rsem,
            device_id={"tm": lax.rem(p + k, slices)},
            device_id_type=MESH,
        )

    def take_start():
        hand_state().wait_recv()
        saved[5] = restrict(stacked(start[...]))

    def term(source, which):
        both = terms[source]
        turned = jnp.concatenate(
            [pltpu.roll(both[:, c * lanes : (c + 1) * lanes], half, 1) for c in range(3)], axis=1
        )
        straight = jnp.where(low_field, 0, 1) == which
        return jnp.where(straight, both, turned)

    @pl.when(chip == 0)
    def _():
        seq[1] = term(0, 0)

    @pl.when(chip > 0)
    def _():
        take_start()
        chain_copy(1).wait_recv()
        both = chain[1]
        turned = jnp.concatenate(
            [pltpu.roll(both[:, c * lanes : (c + 1) * lanes], half, 1) for c in range(3)], axis=1
        )
        seq[2 * chip, : coarse_rows // 2] = jnp.where(low_chain, both, turned)
        seq[2 * chip, coarse_rows // 2 :] = jnp.where(low_chain, turned, both)

    def advance(value, r):
        known = value + term((r + 1) // 2, (r + 1) % 2)
        seq[r + 2] = known + (0.5 * h) * coarse_finish(value, r + 2, c_acc.at[0])

    def open_stage(r):
        value = seq[r + 1]
        value3 = stacked(value)
        coarse_begin(value3, coarse_tab[1], r + 2)
        local(value, value3, coarse_tab, c_acc.at[0])
        return value

    wholes = ((start, saved.at[5]), (v1, saved.at[1]), (v2, saved.at[2]))

    def correct(m):
        whole, part = wholes[m]
        delta = seq[2 * p + m] - part[...]
        coarse_begin(stacked(delta), delta_faces, 2 * slices + 1 + m)
        nodes[m] = whole[...] + prolong(delta)
        local(nodes[m], stacked(nodes[m]), fine_tab, f_acc.at[m])

    def stage(r, carry):
        value = open_stage(r)

        @pl.when((chip == 0) & (r == 0))
        def _():
            take_start()

        @pl.when(r == 2 * p - 1)
        def _():
            correct(0)

        advance(value, r)
        return carry

    lax.fori_loop(jnp.maximum(2 * chip - 1, 0), 2 * p, stage, 0)
    value = open_stage(2 * p)

    @pl.when(p == 0)
    def _():
        saved[5] = restrict(stacked(start[...]))
        correct(0)

    correct(1)
    advance(value, 2 * p)
    chain_on = [(odd == 1) & (p + k < slices) for k in (1, 2)]

    @pl.when(chain_on[0])
    def _():
        node = seq[2 * p + 2]
        chain[0] = jnp.where(low_chain, node[: coarse_rows // 2], node[coarse_rows // 2 :])

    for k in (2, 1):
        @pl.when(chain_on[k - 1])
        def _():
            chain_copy(k).start()

    correct(2)

    @pl.when(p > 0)
    def _():
        hand_halo().wait_recv()

    for m, base_halo in enumerate((start_halo, f_recv.at[1], f_recv.at[2])):
        got = arrive(coarse_part, 2 * slices + 1 + m)
        rates[m] = finish(nodes[m], fine_tab, base_halo[...] + prolong_halo(got), f_acc.at[m])

    @pl.when(sends_term)
    def _():
        term_copy(p, 1).wait_send()

    for k in (2, 1):
        @pl.when(chain_on[k - 1])
        def _():
            chain_copy(k).wait_send()

    @pl.when(p + 1 < slices)
    def _():
        hand_state().wait_send()
        hand_halo().wait_send()

    row = QUAD_WEIGHTS[0]
    v1[...] = nodes[0] + h * (row[0] * rates[0] + row[1] * rates[1] + row[2] * rates[2])
    value3 = begin(v1[...], 3)
    local(v1[...], value3, fine_tab, f_acc.at[0])
    row = QUAD_WEIGHTS[1]
    v2[...] = v1[...] + h * (row[0] * rates[0] + (row[1] - 0.5) * rates[1] + row[2] * rates[2])
    last = v2[...] + (0.5 * h) * finish(v1[...], fine_tab, arrive(fine_part, 3), f_acc.at[0])
    for c in range(3):
        out_ref[c] = last[:, c * lanes : (c + 1) * lanes]


def solution(mesh):
    slices, bricks = mesh.shape["tm"], mesh.shape["space"]

    def shards(initial):
        side, z_length = initial.shape[3], initial.shape[-1]
        lanes = z_length
        half = side // 2
        fine_rows, coarse_rows = side * side, half * half
        fine_points, fine_weights = cheb_tables(FINE)
        coarse_points, coarse_weights = cheb_tables(COARSE)
        down = interp_matrix(fine_points, fine_weights, coarse_points)
        up = interp_matrix(coarse_points, coarse_weights, fine_points)
        spread = lambda m, length: np.kron(np.eye(length // m.shape[1]), m)
        down_side, up_side = spread(down, side), spread(up, half)
        fine_brick = lifted_matrix(FINE, side, False)
        slope_of = [fine_brick[:1] @ up_side, fine_brick[-1:] @ up_side]
        ident = np.eye(half)
        delta_slopes = [np.kron(m, ident) for m in slope_of] + [np.kron(ident, m) for m in slope_of]
        delta_values = face_rows(np.eye(half), half, True)[:4]
        spots = np.eye(8)
        halo_table = np.concatenate(
            [np.kron(spots[j : j + 1], up_side) for d in range(4) for j in (d, 4 + d)]
        )
        up_z = spread(up, z_length // 2).T
        down_z = spread(down, z_length).T
        tables = (
            level_tables(FINE, side, z_length, lanes, False)
            + level_tables(COARSE, half, z_length // 2, lanes, True)
            + [
                left_table(np.kron(down_side, down_side)),
                right_table(np.tile(down_z, (1, 2))),
                left_table(np.kron(up_side, up_side)),
                right_table(padded(up_z, lanes, lanes)),
                left_table(np.concatenate(delta_values + delta_slopes)),
                right_table(np.kron(np.eye(2), up_z)),
                left_table(halo_table),
            ]
        )
        wide = 3 * lanes
        tables = [padded(t, t.shape[0], -(-t.shape[1] // lanes) * lanes) for t in tables]
        bank_width = 2 * wide
        places, heights = [], [0, 0]
        for t in sorted(range(len(tables)), key=lambda t: -tables[t].shape[1]):
            side_by = int(heights[1] < heights[0])
            places.append((t, heights[side_by], side_by * wide))
            for other in range(2) if tables[t].shape[1] > wide else (side_by,):
                heights[other] += tables[t].shape[0]
        places = [place[1:] for place in sorted(places)]
        bank = np.zeros((max(heights) + BANK_SPARE, bank_width), jnp.bfloat16)
        for t, (row, column) in zip(tables, places):
            bank[row : row + t.shape[0], column : column + t.shape[1]] = t
        fine_slots, coarse_slots = 4, 2 * slices + 4
        fine_field = pltpu.VMEM((fine_rows, wide), F32)
        geometry = (slices, bricks, fine_rows, coarse_rows, lanes)
        result = pl.pallas_call(
            functools.partial(kernel, geometry, places),
            out_shape=jax.ShapeDtypeStruct((3, fine_rows, lanes), F32),
            in_specs=[pl.BlockSpec(memory_space=pl.ANY)] * 2,
            out_specs=pl.BlockSpec(memory_space=pltpu.VMEM),
            scratch_shapes=[pltpu.VMEM((3, fine_rows, lanes), F32)]
            + [pltpu.VMEM(t.shape, BF16) for t in tables]
            + [
                pltpu.SemaphoreType.DMA((len(tables) + 1,)),
                fine_field,
                fine_field,
                fine_field,
                pltpu.VMEM((8 * side, wide), F32),
                pltpu.VMEM((3, fine_rows, wide), F32),
                pltpu.VMEM((3, fine_rows, wide), F32),
                pltpu.VMEM((fine_slots, 8 * side, wide), F32),
                pltpu.VMEM((fine_slots, 8 * side, wide), F32),
                pltpu.VMEM((3, 3 * fine_rows, 2 * wide), F32),
                pltpu.VMEM((coarse_slots, 4 * half, wide), F32),
                pltpu.VMEM((coarse_slots, 4 * half, wide), F32),
                pltpu.VMEM((2, 3 * coarse_rows, 2 * wide), F32),
                pltpu.VMEM((2 * slices + 1, coarse_rows, wide), F32),
                pltpu.VMEM((slices, coarse_rows, wide), F32),
                pltpu.VMEM((6, coarse_rows, wide), F32),
                pltpu.SemaphoreType.DMA((fine_slots, 8)),
                pltpu.SemaphoreType.DMA((fine_slots, 8)),
                pltpu.SemaphoreType.DMA((coarse_slots, 4)),
                pltpu.SemaphoreType.DMA((coarse_slots, 4)),
                pltpu.SemaphoreType.DMA((slices,)),
                pltpu.SemaphoreType.DMA((slices,)),
                pltpu.SemaphoreType.DMA((2,)),
                pltpu.SemaphoreType.DMA((2,)),
                pltpu.VMEM((2, coarse_rows // 2, wide), F32),
                pltpu.SemaphoreType.DMA((2,)),
                pltpu.SemaphoreType.DMA,
            ],
            compiler_params=pltpu.CompilerParams(
                collective_id=0, has_side_effects=True, vmem_limit_bytes=VMEM_LIMIT
            ),
        )(initial.reshape(3, fine_rows, lanes), jnp.asarray(bank))
        return result.reshape(initial.shape)

    return jax.shard_map(
        shards,
        mesh=mesh,
        in_specs=(P("tm", None, "space", None, None, None),),
        out_specs=P("tm", None, "space", None, None, None),
        check_vma=False,
    )
```
